512 devices in a mesh: ctx: 32 (over z, x), head: 8 (over y_hi, core), dp: 2 (over y_lo).
Axes of the slice: x: 4, y: 8 (y_hi: 4, y_lo: 2; y = y_hi * 2 + y_lo), z: 8, core: 2. Of those that a mesh axis runs over, the one named last changes fastest.
Arguments:
- latents: bfloat16 [2, 4096, 512], P('dp', 'ctx'), may hold values from -6 to 6
- k_rope: bfloat16 [2, 4096, 64], P('dp', 'ctx'), may hold values from -3 to 3
- q_nope: bfloat16 [2, 4096, 2048], P('dp', 'ctx', 'head'), may hold values from -6 to 6
- q_rope: bfloat16 [2, 4096, 1024], P('dp', 'ctx', 'head')
- grad_out: bfloat16 [2, 4096, 2048], P('dp', 'ctx', 'head'), may hold values from -6 to 6
- saved_out: bfloat16 [2, 4096, 2048], P('dp', 'ctx', 'head'), may hold values from -6 to 6
- w_key: bfloat16 [512, 2048], P(None, 'head'), may hold values from -0.25 to 0.25
- w_value: bfloat16 [512, 2048], P(None, 'head'), may hold values from -0.25 to 0.25
- group_order: int32 [64], replicated, may hold values from 0 to 63, each once
Outputs:
- grad_q_nope: bfloat16 [2, 4096, 2048], P('dp', 'ctx', 'head')
- grad_q_rope: bfloat16 [2, 4096, 1024], P('dp', 'ctx', 'head')
- grad_latents: bfloat16 [2, 4096, 512], P('dp', 'ctx')
- grad_k_rope: bfloat16 [2, 4096, 64], P('dp', 'ctx')
- grad_w_key: float32 [512, 2048], P(('ctx', 'dp'), 'head')
- grad_w_value: float32 [512, 2048], P(('ctx', 'dp'), 'head')
The draws below stay inside these ranges and needn't reach their ends.
Inputs may be any that keep to these rules, and one draw needn't show every extreme that they name: `group_order`: every block number appears once.
All inputs are finite; a program needn't handle non-finite values.
Results may differ from the reference program's by a relative error of at most 0.0095.
Values may be sent and summed in bfloat16 or wider, within the bound.
A program may use at most 64 MiB of HBM per device.

```python
from functools import partial
import jax
import jax.numpy as jnp
from jax import lax

DL = 512
DN = 128
DR = 64
DV = 128
TOK_DEV = 128
HEADS = 16
LENGTH = 4096
SEQS = 2
N_CTX = 32


def shared_rope(key):
    base_rows = jax.random.truncated_normal(key, -3.0, 3.0, (SEQS, LENGTH, DR), jnp.float32)
    return base_rows


def draw_k_rope(key, part):
    base_rows = shared_rope(key)
    return base_rows.astype(jnp.bfloat16)


def draw_q_rope(key, part):
    key = jax.random.fold_in(key, 12)
    first_key = jax.random.fold_in(key, 0)
    drawn = jax.random.normal(first_key, (SEQS, LENGTH, HEADS * DR), jnp.float32)
    return drawn.astype(jnp.bfloat16)


def strengthened(entries, rng, source, target, blocks, factor):
    owner, partner = [(jnp.arange(entries.shape[dim]) // (entries.shape[dim] // blocks)).reshape([-1 if axis == dim else 1 for axis in range(entries.ndim)]) for dim in (source, target)]
    chosen = jax.random.permutation(rng, blocks)[partner]
    strong = (owner == chosen) | (owner == (partner + blocks // 2) % blocks)
    return jnp.where(strong, factor * entries, entries)


def levels(key, extent, cuts, smallest, high):
    factor_of = 1.0
    for dim, parts in cuts:
        steps = jax.random.uniform(jax.random.fold_in(jax.random.fold_in(key, 6), dim), (parts,), jnp.float32, smallest / len(cuts), high / len(cuts))
        factor_of = factor_of * jnp.repeat(jnp.exp(steps), extent[dim] // parts).reshape((-1,) + (1,) * (len(extent) - 1 - dim))
    return factor_of


def noise(key, shape, spread, reach, cuts=(), held_as=jnp.bfloat16):
    gain = levels(key, shape, cuts, -0.22, 0.18) if cuts else 1.0
    array = jax.random.normal(key, shape, jnp.float32) * spread * gain
    return jnp.minimum(jnp.maximum(array, -reach), reach).astype(held_as)


def bell_draw_with(own_key, extent, deviation, limit, cuts, heavy, kind=jnp.bfloat16):
    entries = deviation * jax.random.normal(own_key, extent, jnp.float32)
    if cuts:
        entries = entries * levels(own_key, extent, cuts, -0.22, 0.18)
    return jnp.clip(strengthened(entries, jax.random.fold_in(own_key, 3), *heavy), -limit, limit).astype(kind)


def setup_inputs(seed: int = 0) -> dict:
    arg_keys = jax.random.split(jax.random.key(seed), 10)
    return {
        "latents": bell_draw_with(arg_keys[0], (SEQS, LENGTH, DL), 1.0, 6.0, ((0, 2), (1, 32)), (1, 2, 32, 2.75)),
        "k_rope": draw_k_rope(jax.random.fold_in(arg_keys[9], 71), 0),
        "q_nope": noise(arg_keys[2], (SEQS, LENGTH, HEADS * DN), 1.0, 6.0, ((0, 2), (1, 32), (2, 8))),
        "q_rope": draw_q_rope(jax.random.fold_in(arg_keys[9], 71), 0),
        "grad_out": noise(arg_keys[4], (SEQS, LENGTH, HEADS * DV), 1.0, 6.0, ((0, 2), (1, 32), (2, 8))),
        "saved_out": noise(arg_keys[5], (SEQS, LENGTH, HEADS * DV), 1.0, 6.0, ((0, 2), (1, 32), (2, 8))),
        "w_key": noise(arg_keys[6], (DL, HEADS * DN), DL ** -0.5, 0.25, ((1, 8),)),
        "w_value": noise(arg_keys[7], (DL, HEADS * DV), DL ** -0.5, 0.25, ((1, 8),)),
        "group_order": jax.random.permutation(arg_keys[8], 2 * N_CTX).astype(jnp.int32),
    }


def positions_of(group_order, length, group_rows):
    row_ids = jnp.arange(length, dtype=jnp.int32)
    return group_order[row_ids // group_rows] * group_rows + row_ids % group_rows


def to_heads(matrix, width):
    return matrix.reshape(matrix.shape[0], HEADS, width).transpose(1, 0, 2)


def from_heads(stacked):
    return stacked.transpose(1, 0, 2).reshape(stacked.shape[1], -1)


def head_backward(items, key_rope, position, score_scale):
    query_nope, query_rope, upstream, saved, key_nope, value_rows = items
    scores = (jnp.dot(query_nope, key_nope.T, preferred_element_type=jnp.float32)
              + jnp.dot(query_rope, key_rope.T, preferred_element_type=jnp.float32)) * score_scale
    visible = position[None, :] <= position[:, None]
    masked = jnp.where(visible, scores, -jnp.inf)
    row_top = jnp.max(masked, axis=1, keepdims=True)
    log_total = row_top + jnp.log(jnp.sum(jnp.exp(masked - row_top), axis=1, keepdims=True))
    prob_rows = jnp.where(visible, jnp.exp(scores - log_total), 0.0)
    dprob_rows = jnp.dot(upstream, value_rows.T, preferred_element_type=jnp.float32)
    row_delta = jnp.sum(upstream.astype(jnp.float32) * saved.astype(jnp.float32), axis=1, keepdims=True)
    dscore_rows = (prob_rows * (dprob_rows - row_delta) * score_scale).astype(jnp.bfloat16)
    prob_half = prob_rows.astype(jnp.bfloat16)
    grad_nope = jnp.dot(dscore_rows, key_nope, preferred_element_type=jnp.float32).astype(jnp.bfloat16)
    grad_rope = jnp.dot(dscore_rows, key_rope, preferred_element_type=jnp.float32).astype(jnp.bfloat16)
    grad_key = jnp.dot(dscore_rows.T, query_nope, preferred_element_type=jnp.float32).astype(jnp.bfloat16)
    grad_krope = jnp.dot(dscore_rows.T, query_rope, preferred_element_type=jnp.float32)
    grad_value = jnp.dot(prob_half.T, upstream, preferred_element_type=jnp.float32).astype(jnp.bfloat16)
    return grad_nope, grad_rope, grad_key, grad_krope, grad_value


def reference(latents, k_rope, q_nope, q_rope, grad_out, saved_out, w_key, w_value, group_order):
    score_scale = (DN + DR) ** -0.5
    position = positions_of(group_order, LENGTH, TOK_DEV // 2)
    out_nope, out_rope, out_latent, out_krope = [], [], [], []
    grad_wkey = jnp.zeros((DL, HEADS * DN), jnp.float32)
    grad_wvalue = jnp.zeros((DL, HEADS * DV), jnp.float32)
    for seq_index in range(SEQS):
        key_nope = jnp.dot(latents[seq_index], w_key, preferred_element_type=jnp.float32).astype(jnp.bfloat16)
        value_rows = jnp.dot(latents[seq_index], w_value, preferred_element_type=jnp.float32).astype(jnp.bfloat16)
        items = (to_heads(q_nope[seq_index], DN), to_heads(q_rope[seq_index], DR),
                 to_heads(grad_out[seq_index], DV), to_heads(saved_out[seq_index], DV),
                 to_heads(key_nope, DN), to_heads(value_rows, DV))
        per_head = lax.map(partial(head_backward, key_rope=k_rope[seq_index], position=position,
                                   score_scale=score_scale), items)
        grad_nope, grad_rope, grad_key, grad_krope, grad_value = per_head
        key_flat = from_heads(grad_key)
        value_flat = from_heads(grad_value)
        latent_grad = (jnp.dot(key_flat, w_key.T, preferred_element_type=jnp.float32)
                       + jnp.dot(value_flat, w_value.T, preferred_element_type=jnp.float32))
        out_nope.append(from_heads(grad_nope))
        out_rope.append(from_heads(grad_rope))
        out_latent.append(latent_grad.astype(jnp.bfloat16))
        out_krope.append(jnp.sum(grad_krope, axis=0).astype(jnp.bfloat16))
        grad_wkey = grad_wkey + jnp.dot(latents[seq_index].T, key_flat, preferred_element_type=jnp.float32)
        grad_wvalue = grad_wvalue + jnp.dot(latents[seq_index].T, value_flat, preferred_element_type=jnp.float32)
    return (jnp.stack(out_nope), jnp.stack(out_rope), jnp.stack(out_latent), jnp.stack(out_krope),
            grad_wkey, grad_wvalue)
```

```python
import functools
import math

import jax
import jax.numpy as jnp
from jax import lax
from jax.experimental import pallas as pl
from jax.experimental.pallas import tpu as pltpu
from jax.sharding import PartitionSpec as P

DL = 512
DN = 128
DR = 64
DV = 128
NX = 4
CORES = 2
HALF_GROUP = 64

MESH = pl.DeviceIdType.MESH
MASKED = -1.5e38
FLOOR = -1.0e38
F32 = jnp.float32
BF16 = jnp.bfloat16

NT = (((1,), (1,)), ((), ()))


def dot(a, b):
    return jnp.dot(a, b, preferred_element_type=F32)


def dot_nt(a, b):
    return lax.dot_general(a, b, NT, preferred_element_type=F32)


def ring_offset(r, n):
    odd = lax.rem(r, 2)
    return odd * lax.div(r + 1, 2) + (1 - odd) * (n - lax.div(r, 2))


def kernel(
    nz, nyh, tok,
    lat_in, kr_in, qn_in, qr_in, go_in, so_in, wk_in, wv_in, order,
    gqn_out, gqr_out, gl_out, gkr_out, gwk_out, gwv_out,
    lat, krs, q, saved, w, delta, qpos, qcat, qgo, latt, keyst,
    pexp, dsx, mscr, lscr, stats, dsall, gall,
    glsend, glsib, glz, glzr, tot, ychunk, yrecv, final,
    gqf, gqb, gqr, gwf, gwb, gwr, gwzf, gwzb, gwzr, gwdf, gwdr,
    local_sem, lat_s, lat_r, fwd_s, fwd_r, q_s, q_r, de_s, de_r, st_s, st_r,
    sib_s, sib_r, glz_s, glz_r, gq_s, gq_r, gwx_s, gwx_r, gwz_s, gwz_r,
    y_s, y_r, fin_s, fin_r, dp_s, dp_r,
):
    ctx = lax.axis_index("ctx")
    head = lax.axis_index("head")
    dp = lax.axis_index("dp")
    z, x = lax.div(ctx, NX), lax.rem(ctx, NX)
    y, core = lax.div(head, CORES), lax.rem(head, CORES)
    heads = nyh * CORES
    half = tok // CORES
    queries = NX * tok
    keys = nz * tok
    score_scale = (DN + DR) ** -0.5
    log2_scale = score_scale * math.log2(math.e)

    def at_z(z_peer):
        return {"ctx": z_peer * NX + x, "head": head, "dp": dp}

    def at_x(x_peer):
        return {"ctx": z * NX + x_peer, "head": head, "dp": dp}

    def at_head(peer):
        return {"ctx": ctx, "head": peer, "dp": dp}

    sibling = at_head(y * CORES + (1 - core))
    other_dp = {"ctx": ctx, "head": head, "dp": 1 - dp}

    def remote(src, dst, send, recv, device):
        return pltpu.make_async_remote_copy(
            src_ref=src, dst_ref=dst, send_sem=send, recv_sem=recv,
            device_id=device, device_id_type=MESH,
        )

    z_peers = [lax.rem(z + (k if k <= nz // 2 else k), nz) for k in range(1, nz)]
    x_peers = [lax.rem(x + k, NX) for k in range(1, NX)]
    y_peers = [lax.rem(y + k, nyh) for k in range(1, nyh)]
    head_peers = [lax.rem(head + k, heads) for k in range(1, heads)]

    def z_at(r):
        return lax.rem(z + ring_offset(r, nz), nz)

    local = [
        pltpu.make_async_copy(lat_in.at[0], lat.at[z, :, pl.ds(0, DL)], local_sem.at[0]),
        pltpu.make_async_copy(kr_in.at[0], krs, local_sem.at[1]),
        pltpu.make_async_copy(qn_in.at[0], q.at[x, :, pl.ds(0, 2 * DN)], local_sem.at[2]),
        pltpu.make_async_copy(qr_in.at[0], q.at[x, :, pl.ds(2 * DN, 2 * DR)], local_sem.at[3]),
        pltpu.make_async_copy(
            go_in.at[0], q.at[x, :, pl.ds(2 * DN + 2 * DR, 2 * DV)], local_sem.at[4]
        ),
        pltpu.make_async_copy(so_in.at[0], saved, local_sem.at[5]),
        pltpu.make_async_copy(wk_in, w.at[:, pl.ds(0, 2 * DN)], local_sem.at[6]),
        pltpu.make_async_copy(wv_in, w.at[:, pl.ds(2 * DN, 2 * DV)], local_sem.at[7]),
    ]
    for copy in local:
        copy.start()

    barrier = pltpu.get_barrier_semaphore()
    targets = (
        [at_z(p) for p in z_peers] + [at_x(p) for p in x_peers]
        + [at_head(p) for p in head_peers] + [other_dp]
    )
    for target in targets:
        pl.semaphore_signal(barrier, inc=1, device_id=target, device_id_type=MESH)
    for copy in local:
        copy.wait()
    rope_lanes = jnp.concatenate([krs[...], jnp.zeros((tok, DR), BF16)], axis=1)
    lat[z, :, DL:] = rope_lanes
    pl.semaphore_wait(barrier, len(targets))

    own_rows = pl.ds(pl.multiple_of(core * half, half), half)
    other_rows = pl.ds(pl.multiple_of((1 - core) * half, half), half)

    def lat_copy(k, src_z, dst_z):
        return remote(
            lat.at[src_z, own_rows], lat.at[src_z, own_rows], lat_s.at[k], lat_r.at[src_z],
            at_z(dst_z),
        )

    def forward_copy(src_z):
        return remote(
            lat.at[src_z, own_rows], lat.at[src_z, own_rows], fwd_s.at[src_z], fwd_r.at[src_z],
            sibling,
        )

    def forward_arrival(src_z):
        return remote(
            lat.at[src_z, other_rows], lat.at[src_z, other_rows], fwd_s.at[src_z],
            fwd_r.at[src_z], sibling,
        )

    q_copies = [
        remote(q.at[x], q.at[x], q_s.at[k], q_r.at[x], at_x(p)) for k, p in enumerate(x_peers)
    ]
    lat_copies = [lat_copy(r - 1, z, z_at(r)) for r in range(1, nz)]
    for k in range(max(len(q_copies), len(lat_copies))):
        if k < len(q_copies):
            q_copies[k].start()
        if k < len(lat_copies):
            lat_copies[k].start()

    upstream = q[x, :, 2 * DN + 2 * DR:].astype(F32)
    product = (upstream * saved[...].astype(F32)).T
    delta[x, 0:1, :] = jnp.sum(product[:DV], axis=0, keepdims=True)
    delta[x, 1:2, :] = jnp.sum(product[DV:], axis=0, keepdims=True)
    delta_copies = [
        remote(delta.at[x], delta.at[x], de_s.at[k], de_r.at[x], at_x(p))
        for k, p in enumerate(x_peers)
    ]
    for copy in delta_copies:
        copy.start()

    lane = lax.broadcasted_iota(jnp.int32, (1, tok), 1)
    for p in range(NX):
        first = 2 * (z * NX + p)
        qpos[0:1, p * tok:(p + 1) * tok] = jnp.where(
            lane < HALF_GROUP,
            order[first] * HALF_GROUP + lane,
            order[first + 1] * HALF_GROUP + lane - HALF_GROUP,
        )

    for p in x_peers:
        remote(q.at[p], q.at[p], q_s.at[0], q_r.at[p], at_x(p)).wait_recv()
        remote(delta.at[p], delta.at[p], de_s.at[0], de_r.at[p], at_x(p)).wait_recv()
    for p in range(NX):
        rows = pl.ds(p * tok, tok)
        for h in range(2):
            qcat[h, rows, 0:DN] = q[p, :, h * DN:(h + 1) * DN]
            qcat[h, rows, DN:] = q[p, :, 2 * DN:2 * DN + 2 * DR]
            qgo[h, rows, :] = q[p, :, 2 * DN + 2 * DR + h * DV:2 * DN + 2 * DR + (h + 1) * DV]

    def first_pass(r, carry):
        block = z_at(r)

        @pl.when(r < nz - 1)
        def _():
            coming = z_at(r + 1)
            lat_copy(0, coming, coming).wait_recv()
            forward_copy(coming).start()

        @pl.when(r > 0)
        def _():
            forward_arrival(block).wait_recv()

        latents = lat[block, :, 0:DL]
        rope0 = lat[block, :, DL:]
        rope1 = jnp.concatenate([rope0[:, DR:], rope0[:, :DR]], axis=1)
        projected = dot(latents, w[...]).astype(BF16)
        columns = pl.ds(pl.multiple_of(r * tok, tok), tok)
        latt[:, columns] = latents.T
        first = 2 * (block * NX + x)
        row = lax.broadcasted_iota(jnp.int32, (HALF_GROUP, queries), 0)
        where_q = qpos[0:1, :]
        seen = jnp.concatenate(
            [row <= where_q - order[first + g] * HALF_GROUP for g in range(2)], axis=0
        )
        for h in range(2):
            key = jnp.concatenate(
                [projected[:, h * DN:(h + 1) * DN], rope0 if h == 0 else rope1], axis=1
            )
            keyst[h, :, columns] = key.T
            scores = jnp.where(seen, dot_nt(key, qcat[h]) * log2_scale, MASKED)
            top = jnp.maximum(jnp.max(scores, axis=0, keepdims=True), FLOOR)
            weight = jnp.exp2(scores - top)
            mscr[h, r] = top
            lscr[h, r] = jnp.sum(weight, axis=0, keepdims=True)
            dprobs = dot_nt(projected[:, 2 * DN + h * DV:2 * DN + (h + 1) * DV], qgo[h])
            row_delta = jnp.concatenate([delta[p, h:h + 1, :] for p in range(NX)], axis=1)
            pexp[h, r] = weight
            dsx[h, r] = weight * (dprobs - row_delta)
        return carry

    lax.fori_loop(0, nz, first_pass, 0)

    for h in range(2):
        top = mscr[h, 0]
        for r in range(1, nz):
            top = jnp.maximum(top, mscr[h, r])
        total = jnp.zeros_like(top)
        for r in range(nz):
            total += lscr[h, r] * jnp.exp2(mscr[h, r] - top)
        stats[x, 2 * h:2 * h + 1, :] = top
        stats[x, 2 * h + 1:2 * h + 2, :] = total
    stat_copies = [
        remote(stats.at[x], stats.at[x], st_s.at[k], st_r.at[x], at_x(p))
        for k, p in enumerate(x_peers)
    ]
    for copy in stat_copies:
        copy.start()
    for p in x_peers:
        remote(stats.at[p], stats.at[p], st_s.at[0], st_r.at[p], at_x(p)).wait_recv()
    log_total = []
    for h in range(2):
        top = stats[0, 2 * h:2 * h + 1, :]
        for p in range(1, NX):
            top = jnp.maximum(top, stats[p, 2 * h:2 * h + 1, :])
        total = jnp.zeros_like(top)
        for p in range(NX):
            total += stats[p, 2 * h + 1:2 * h + 2, :] * jnp.exp2(
                stats[p, 2 * h:2 * h + 1, :] - top
            )
        log_total.append(top + jnp.log2(total))

    def sib_copy(r):
        return remote(glsend.at[r, other_rows], glsib.at[r], sib_s.at[r], sib_r.at[r], sibling)

    def glz_copy(r):
        return remote(glz.at[r], glzr.at[z], glz_s.at[r], glz_r.at[z], at_z(z_at(r)))

    def chip_sum(r):
        sib_copy(r).wait_recv()
        return glsend[r, own_rows, :].astype(F32) + glsib[r].astype(F32)

    def second_pass(step, carry):
        r = nz - 1 - step
        rows = pl.ds(pl.multiple_of(r * tok, tok), tok)
        key_parts, value_parts, rope_parts = [], [], []
        for h in range(2):
            factor = jnp.exp2(mscr[h, r] - carry[h])
            probs = (pexp[h, r] * factor).astype(BF16)
            dscores = (dsx[h, r] * (factor * score_scale)).astype(BF16)
            dsall[h, rows, :] = dscores
            joint = dot(dscores, qcat[h])
            key_parts.append(joint[:, :DN].astype(BF16))
            rope_parts.append(joint[:, DN:])
            value_parts.append(dot(probs, qgo[h]).astype(BF16))
        grads = jnp.concatenate(key_parts + value_parts, axis=1)
        gall[rows, :] = grads
        ropes = jnp.where(
            lax.broadcasted_iota(jnp.int32, (tok, 2 * DR), 1) < DR, rope_parts[0], rope_parts[1]
        )
        glsend[r, :, 0:DL] = dot_nt(grads, w[...]).astype(BF16)
        glsend[r, :, DL:] = ropes.astype(BF16)
        sib_copy(r).start()

        @pl.when(step > 0)
        def _():
            glz[r + 1] = chip_sum(r + 1).astype(BF16)
            glz_copy(r + 1).start()

        return carry

    lax.fori_loop(0, nz, second_pass, tuple(log_total))

    parts = [dot(keyst[h], dsall[h]) for h in range(2)]
    stacked = jnp.concatenate(
        [parts[0][:DN], parts[1][:DN], parts[0][DN:] + parts[1][DN:]], axis=0
    )
    turned = stacked.T
    gqb[...] = turned.astype(BF16).reshape(gqb.shape)
    gqf[...] = turned
    gq_copies = [
        remote(gqb.at[p], gqr.at[x], gq_s.at[k], gq_r.at[x], at_x(p))
        for k, p in enumerate(x_peers)
    ]
    for copy in gq_copies:
        copy.start()

    sub = DL // (nz * NX)
    gwf[...] = dot(latt[...], gall[...]).reshape(gwf.shape)
    for p in range(NX):
        gwb[p] = gwf[:, p].astype(BF16)
    gwx_copies = [
        remote(gwb.at[p], gwr.at[x], gwx_s.at[k], gwx_r.at[x], at_x(p))
        for k, p in enumerate(x_peers)
    ]
    for copy in gwx_copies:
        copy.start()

    total = chip_sum(0)
    for k in range(1, nz):
        p = z_at(k)
        remote(glz.at[0], glzr.at[p], glz_s.at[0], glz_r.at[p], at_z(p)).wait_recv()
        total += glzr[p].astype(F32)
    tot[...] = total.reshape(tot.shape)
    ychunk[...] = total.astype(BF16).reshape(ychunk.shape)
    y_copies = [
        remote(ychunk.at[p], yrecv.at[y], y_s.at[k], y_r.at[y], at_head(p * CORES + core))
        for k, p in enumerate(y_peers)
    ]
    for copy in y_copies:
        copy.start()

    own_tok = pl.ds(pl.multiple_of(x * tok, tok), tok)
    mine = gqf[own_tok, :]
    for p in x_peers:
        remote(gqb.at[0], gqr.at[p], gq_s.at[0], gq_r.at[p], at_x(p)).wait_recv()
        mine += gqr[p].astype(F32)
    gqn_out[0] = mine[:, :2 * DN].astype(BF16)
    gqr_out[0] = mine[:, 2 * DN:].astype(BF16)

    part = gwf[:, x]
    for p in x_peers:
        remote(gwb.at[0], gwr.at[p], gwx_s.at[0], gwx_r.at[p], at_x(p)).wait_recv()
        part += gwr[p].astype(F32)
    gwzf[...] = part
    gwzb[...] = part.astype(BF16)
    gwz_copies = [
        remote(gwzb.at[z_at(r)], gwzr.at[z], gwz_s.at[r - 1], gwz_r.at[z], at_z(z_at(r)))
        for r in range(1, nz)
    ]
    for copy in gwz_copies:
        copy.start()

    mine = tot[y]
    for p in y_peers:
        remote(
            ychunk.at[0], yrecv.at[p], y_s.at[0], y_r.at[p], at_head(p * CORES + core)
        ).wait_recv()
        mine += yrecv[p].astype(F32)
    folded = mine[:, DL:] + jnp.concatenate([mine[:, DL + DR:], mine[:, DL:DL + DR]], axis=1)
    slot = core * nyh + y
    final[slot, :, 0:DL] = mine[:, :DL].astype(BF16)
    final[slot, :, DL:] = folded.astype(BF16)
    fin_copies = [
        remote(final.at[slot], final.at[slot], fin_s.at[k], fin_r.at[slot], at_head(p))
        for k, p in enumerate(head_peers)
    ]
    for copy in fin_copies:
        copy.start()

    part = gwzf[z]
    for r in range(1, nz):
        p = z_at(r)
        remote(gwzb.at[0], gwzr.at[p], gwz_s.at[0], gwz_r.at[p], at_z(p)).wait_recv()
        part += gwzr[p].astype(F32)
    gwdf[...] = part.reshape(gwdf.shape)
    dp_copy = remote(gwdf.at[1 - dp], gwdr, dp_s.at[0], dp_r.at[0], other_dp)
    dp_copy.start()

    for p in head_peers:
        from_slot = lax.rem(p, CORES) * nyh + lax.div(p, CORES)
        remote(
            final.at[from_slot], final.at[from_slot], fin_s.at[0], fin_r.at[from_slot], at_head(p)
        ).wait_recv()
    rows_16 = half // nyh
    for k in range(heads):
        gl_out[0, k * rows_16:(k + 1) * rows_16, :] = final[k, :, 0:DL]
        gkr_out[0, k * rows_16:(k + 1) * rows_16, :] = final[k, :, DL:DL + DR]

    dp_copy.wait_recv()
    summed = gwdf[dp] + gwdr[...]
    gwk_out[...] = summed[:, :2 * DN]
    gwv_out[...] = summed[:, 2 * DN:]

    for copy in (
        q_copies + lat_copies + delta_copies + stat_copies + gq_copies + gwx_copies + y_copies
        + gwz_copies + fin_copies + [dp_copy]
    ):
        copy.wait_send()

    def drain(r, carry):
        sib_copy(r).wait_send()

        @pl.when(r > 0)
        def _():
            forward_copy(z_at(r)).wait_send()
            glz_copy(r).wait_send()

        return carry

    lax.fori_loop(0, nz, drain, 0)


def solution(mesh):
    nz = mesh.shape["ctx"] // NX
    nyh = mesh.shape["head"] // CORES

    def shards(*args):
        tok = args[0].shape[1]
        half = tok // CORES
        queries, keys = NX * tok, nz * tok
        sub = DL // (nz * NX)
        rows_y = half // nyh
        wide = DL + 2 * DR
        q_wide = 2 * DN + 2 * DR + 2 * DV
        cols = 2 * DN + 2 * DV
        any_spec = pl.BlockSpec(memory_space=pl.ANY)
        vmem = pl.BlockSpec(memory_space=pltpu.VMEM)
        dma = pltpu.SemaphoreType.DMA
        heads = nyh * CORES
        scratch = [
            pltpu.VMEM((nz, tok, wide), BF16),
            pltpu.VMEM((tok, DR), BF16),
            pltpu.VMEM((NX, tok, q_wide), BF16),
            pltpu.VMEM((tok, 2 * DV), BF16),
            pltpu.VMEM((DL, cols), BF16),
            pltpu.VMEM((NX, 8, tok), F32),
            pltpu.VMEM((8, queries), jnp.int32),
            pltpu.VMEM((2, queries, DN + 2 * DR), BF16),
            pltpu.VMEM((2, queries, DV), BF16),
            pltpu.VMEM((DL, keys), BF16),
            pltpu.VMEM((2, DN + 2 * DR, keys), BF16),
            pltpu.VMEM((2, nz, tok, queries), F32),
            pltpu.VMEM((2, nz, tok, queries), F32),
            pltpu.VMEM((2, nz, 1, queries), F32),
            pltpu.VMEM((2, nz, 1, queries), F32),
            pltpu.VMEM((NX, 8, queries), F32),
            pltpu.VMEM((2, keys, queries), BF16),
            pltpu.VMEM((keys, cols), BF16),
            pltpu.VMEM((nz, tok, wide), BF16),
            pltpu.VMEM((nz, half, wide), BF16),
            pltpu.VMEM((nz, half, wide), BF16),
            pltpu.VMEM((nz, half, wide), BF16),
            pltpu.VMEM((nyh, rows_y, wide), F32),
            pltpu.VMEM((nyh, rows_y, wide), BF16),
            pltpu.VMEM((nyh, rows_y, wide), BF16),
            pltpu.VMEM((heads, rows_y, wide), BF16),
            pltpu.VMEM((queries, 2 * DN + 2 * DR), F32),
            pltpu.VMEM((NX, tok, 2 * DN + 2 * DR), BF16),
            pltpu.VMEM((NX, tok, 2 * DN + 2 * DR), BF16),
            pltpu.VMEM((nz, NX, sub, cols), F32),
            pltpu.VMEM((NX, nz, sub, cols), BF16),
            pltpu.VMEM((NX, nz, sub, cols), BF16),
            pltpu.VMEM((nz, sub, cols), F32),
            pltpu.VMEM((nz, sub, cols), BF16),
            pltpu.VMEM((nz, sub, cols), BF16),
            pltpu.VMEM((2, sub // 2, cols), F32),
            pltpu.VMEM((sub // 2, cols), F32),
            dma((8,)),
            dma((nz,)), dma((nz,)), dma((nz,)), dma((nz,)),
            dma((NX,)), dma((NX,)), dma((NX,)), dma((NX,)), dma((NX,)), dma((NX,)),
            dma((nz,)), dma((nz,)), dma((nz,)), dma((nz,)),
            dma((NX,)), dma((NX,)), dma((NX,)), dma((NX,)), dma((nz,)), dma((nz,)),
            dma((nyh,)), dma((nyh,)), dma((heads,)), dma((heads,)), dma((1,)), dma((1,)),
        ]
        return pl.pallas_call(
            functools.partial(kernel, nz, nyh, tok),
            out_shape=(
                jax.ShapeDtypeStruct((1, tok, 2 * DN), BF16),
                jax.ShapeDtypeStruct((1, tok, 2 * DR), BF16),
                jax.ShapeDtypeStruct((1, tok, DL), BF16),
                jax.ShapeDtypeStruct((1, tok, DR), BF16),
                jax.ShapeDtypeStruct((sub // 2, 2 * DN), F32),
                jax.ShapeDtypeStruct((sub // 2, 2 * DV), F32),
            ),
            in_specs=[any_spec] * 8 + [pl.BlockSpec(memory_space=pltpu.SMEM)],
            out_specs=(vmem,) * 6,
            scratch_shapes=scratch,
            compiler_params=pltpu.CompilerParams(
                collective_id=0, has_side_effects=True, vmem_limit_bytes=56 * 1024 * 1024
            ),
        )(*args)

    return jax.shard_map(
        shards,
        mesh=mesh,
        in_specs=(
            P("dp", "ctx", None),
            P("dp", "ctx", None),
            P("dp", "ctx", "head"),
            P("dp", "ctx", "head"),
            P("dp", "ctx", "head"),
            P("dp", "ctx", "head"),
            P(None, "head"),
            P(None, "head"),
            P(),
        ),
        out_specs=(
            P("dp", "ctx", "head"),
            P("dp", "ctx", "head"),
            P("dp", "ctx", None),
            P("dp", "ctx", None),
            P(("ctx", "dp"), "head"),
            P(("ctx", "dp"), "head"),
        ),
        check_vma=False,
    )
```

```python
import functools
import math

import jax
import jax.numpy as jnp
from jax import lax
from jax.experimental import pallas as pl
from jax.experimental.pallas import tpu as pltpu
from jax.sharding import PartitionSpec as P

DL = 512
DN = 128
DR = 64
DV = 128
NX = 4
CORES = 2
HALF_GROUP = 64

MESH = pl.DeviceIdType.MESH
MASKED = -1.5e38
FLOOR = -1.0e38
F32 = jnp.float32
BF16 = jnp.bfloat16

NT = (((1,), (1,)), ((), ()))


def dot(a, b):
    return jnp.dot(a, b, preferred_element_type=F32)


def dot_nt(a, b):
    return lax.dot_general(a, b, NT, preferred_element_type=F32)


def ring_offset(r, n):
    odd = lax.rem(r, 2)
    return odd * lax.div(r + 1, 2) + (1 - odd) * (n - lax.div(r, 2))


def kernel(
    nz, nyh, tok,
    lat_in, kr_in, qn_in, qr_in, go_in, so_in, wk_in, wv_in, order,
    gqn_out, gqr_out, gl_out, gkr_out, gwk_out, gwv_out,
    lat, krs, q, saved, w, delta, qpos, qcat, qgo, latt, keyst,
    pexp, dsx, mscr, lscr, stats, dsall, gall,
    glsend, glsib, glz, glzr, tot, ychunk, yrecv, final,
    gqf, gqb, gqr, gwf, gwb, gwr, gwzf, gwzb, gwzr, gwdf, gwdr,
    gqn_v, gqr_v, gl_v, gkr_v, gwk_v, gwv_v,
    local_sem, out_sem, lat_s, lat_r, fwd_s, fwd_r, q_s, q_r, de_s, de_r, st_s, st_r,
    sib_s, sib_r, glz_s, glz_r, gq_s, gq_r, gwx_s, gwx_r, gwz_s, gwz_r,
    y_s, y_r, fin_s, fin_r, dp_s, dp_r,
):
    ctx = lax.axis_index("ctx")
    head = lax.axis_index("head")
    dp = lax.axis_index("dp")
    z, x = lax.div(ctx, NX), lax.rem(ctx, NX)
    y, core = lax.div(head, CORES), lax.rem(head, CORES)
    heads = nyh * CORES
    half = tok // CORES
    queries = NX * tok
    keys = nz * tok
    score_scale = (DN + DR) ** -0.5
    log2_scale = score_scale * math.log2(math.e)

    def at_z(z_peer):
        return {"ctx": z_peer * NX + x, "head": head, "dp": dp}

    def at_x(x_peer):
        return {"ctx": z * NX + x_peer, "head": head, "dp": dp}

    def at_head(peer):
        return {"ctx": ctx, "head": peer, "dp": dp}

    sibling = at_head(y * CORES + (1 - core))
    other_dp = {"ctx": ctx, "head": head, "dp": 1 - dp}

    def remote(src, dst, send, recv, device):
        return pltpu.make_async_remote_copy(
            src_ref=src, dst_ref=dst, send_sem=send, recv_sem=recv,
            device_id=device, device_id_type=MESH,
        )

    z_peers = [lax.rem(z + (k if k <= nz // 2 else k), nz) for k in range(1, nz)]
    x_peers = [lax.rem(x + k, NX) for k in range(1, NX)]
    y_peers = [lax.rem(y + k, nyh) for k in range(1, nyh)]
    head_peers = [lax.rem(head + k, heads) for k in range(1, heads)]

    def z_at(r):
        return lax.rem(z + ring_offset(r, nz), nz)

    local = [
        pltpu.make_async_copy(lat_in.at[0], lat.at[z, :, pl.ds(0, DL)], local_sem.at[0]),
        pltpu.make_async_copy(kr_in.at[0], krs, local_sem.at[1]),
        pltpu.make_async_copy(qn_in.at[0], q.at[x, :, pl.ds(0, 2 * DN)], local_sem.at[2]),
        pltpu.make_async_copy(qr_in.at[0], q.at[x, :, pl.ds(2 * DN, 2 * DR)], local_sem.at[3]),
        pltpu.make_async_copy(
            go_in.at[0], q.at[x, :, pl.ds(2 * DN + 2 * DR, 2 * DV)], local_sem.at[4]
        ),
        pltpu.make_async_copy(so_in.at[0], saved, local_sem.at[5]),
        pltpu.make_async_copy(wk_in, w.at[:, pl.ds(0, 2 * DN)], local_sem.at[6]),
        pltpu.make_async_copy(wv_in, w.at[:, pl.ds(2 * DN, 2 * DV)], local_sem.at[7]),
    ]
    for copy in local:
        copy.start()

    barrier = pltpu.get_barrier_semaphore()
    targets = (
        [at_z(p) for p in z_peers] + [at_x(p) for p in x_peers]
        + [at_head(p) for p in head_peers] + [other_dp]
    )
    for target in targets:
        pl.semaphore_signal(barrier, inc=1, device_id=target, device_id_type=MESH)
    for copy in local:
        copy.wait()
    rope_lanes = jnp.concatenate([krs[...].T, jnp.zeros((tok, DR), BF16)], axis=1)
    lat[z, :, DL:] = rope_lanes
    pl.semaphore_wait(barrier, len(targets))

    own_rows = pl.ds(pl.multiple_of(core * half, half), half)
    other_rows = pl.ds(pl.multiple_of((1 - core) * half, half), half)

    def lat_copy(k, src_z, dst_z):
        return remote(
            lat.at[src_z, own_rows], lat.at[src_z, own_rows], lat_s.at[k], lat_r.at[src_z],
            at_z(dst_z),
        )

    def forward_copy(src_z):
        return remote(
            lat.at[src_z, own_rows], lat.at[src_z, own_rows], fwd_s.at[src_z], fwd_r.at[src_z],
            sibling,
        )

    def forward_arrival(src_z):
        return remote(
            lat.at[src_z, other_rows], lat.at[src_z, other_rows], fwd_s.at[src_z],
            fwd_r.at[src_z], sibling,
        )

    q_copies = [
        remote(q.at[x], q.at[x], q_s.at[k], q_r.at[x], at_x(p)) for k, p in enumerate(x_peers)
    ]
    lat_copies = [lat_copy(r - 1, z, z_at(r)) for r in range(1, nz)]
    for k in range(max(len(q_copies), len(lat_copies))):
        if k < len(q_copies):
            q_copies[k].start()
        if k < len(lat_copies):
            lat_copies[k].start()

    upstream = q[x, :, 2 * DN + 2 * DR:].astype(F32)
    product = (upstream * saved[...].astype(F32)).T
    delta[x, 0:1, :] = jnp.sum(product[:DV], axis=0, keepdims=True)
    delta[x, 1:2, :] = jnp.sum(product[DV:], axis=0, keepdims=True)
    delta_copies = [
        remote(delta.at[x], delta.at[x], de_s.at[k], de_r.at[x], at_x(p))
        for k, p in enumerate(x_peers)
    ]
    for copy in delta_copies:
        copy.start()

    lane = lax.broadcasted_iota(jnp.int32, (1, tok), 1)
    for p in range(NX):
        first = 2 * (z * NX + p)
        qpos[0:1, p * tok:(p + 1) * tok] = jnp.where(
            lane < HALF_GROUP,
            order[first] * HALF_GROUP + lane,
            order[first + 1] * HALF_GROUP + lane - HALF_GROUP,
        )

    for p in x_peers:
        remote(q.at[p], q.at[p], q_s.at[0], q_r.at[p], at_x(p)).wait_recv()
        remote(delta.at[p], delta.at[p], de_s.at[0], de_r.at[p], at_x(p)).wait_recv()
    for p in range(NX):
        rows = pl.ds(p * tok, tok)
        for h in range(2):
            qcat[h, rows, 0:DN] = q[p, :, h * DN:(h + 1) * DN]
            qcat[h, rows, DN:] = q[p, :, 2 * DN:2 * DN + 2 * DR]
            qgo[h, rows, :] = q[p, :, 2 * DN + 2 * DR + h * DV:2 * DN + 2 * DR + (h + 1) * DV]

    def first_pass(r, carry):
        block = z_at(r)

        @pl.when(r < nz - 1)
        def _():
            coming = z_at(r + 1)
            lat_copy(0, coming, coming).wait_recv()
            forward_copy(coming).start()

        @pl.when(r > 0)
        def _():
            forward_arrival(block).wait_recv()

        latents = lat[block, :, 0:DL]
        rope0 = lat[block, :, DL:]
        rope1 = jnp.concatenate([rope0[:, DR:], rope0[:, :DR]], axis=1)
        projected = dot(latents, w[...]).astype(BF16)
        columns = pl.ds(pl.multiple_of(r * tok, tok), tok)
        latt[:, columns] = latents.T
        first = 2 * (block * NX + x)
        row = lax.broadcasted_iota(jnp.int32, (HALF_GROUP, queries), 0)
        where_q = qpos[0:1, :]
        seen = jnp.concatenate(
            [row <= where_q - order[first + g] * HALF_GROUP for g in range(2)], axis=0
        )
        for h in range(2):
            key = jnp.concatenate(
                [projected[:, h * DN:(h + 1) * DN], rope0 if h == 0 else rope1], axis=1
            )
            keyst[h, :, columns] = key.T
            scores = jnp.where(seen, dot_nt(key, qcat[h]) * log2_scale, MASKED)
            top = jnp.maximum(jnp.max(scores, axis=0, keepdims=True), FLOOR)
            weight = jnp.exp2(scores - top)
            mscr[h, r] = top
            lscr[h, r] = jnp.sum(weight, axis=0, keepdims=True)
            dprobs = dot_nt(projected[:, 2 * DN + h * DV:2 * DN + (h + 1) * DV], qgo[h])
            row_delta = jnp.concatenate([delta[p, h:h + 1, :] for p in range(NX)], axis=1)
            pexp[h, r] = weight
            dsx[h, r] = weight * (dprobs - row_delta)
        return carry

    lax.fori_loop(0, nz, first_pass, 0)

    for h in range(2):
        top = mscr[h, 0]
        for r in range(1, nz):
            top = jnp.maximum(top, mscr[h, r])
        total = jnp.zeros_like(top)
        for r in range(nz):
            total += lscr[h, r] * jnp.exp2(mscr[h, r] - top)
        stats[x, 2 * h:2 * h + 1, :] = top
        stats[x, 2 * h + 1:2 * h + 2, :] = total
    stat_copies = [
        remote(stats.at[x], stats.at[x], st_s.at[k], st_r.at[x], at_x(p))
        for k, p in enumerate(x_peers)
    ]
    for copy in stat_copies:
        copy.start()
    for p in x_peers:
        remote(stats.at[p], stats.at[p], st_s.at[0], st_r.at[p], at_x(p)).wait_recv()
    log_total = []
    for h in range(2):
        top = stats[0, 2 * h:2 * h + 1, :]
        for p in range(1, NX):
            top = jnp.maximum(top, stats[p, 2 * h:2 * h + 1, :])
        total = jnp.zeros_like(top)
        for p in range(NX):
            total += stats[p, 2 * h + 1:2 * h + 2, :] * jnp.exp2(
                stats[p, 2 * h:2 * h + 1, :] - top
            )
        log_total.append(top + jnp.log2(total))

    def sib_copy(r):
        return remote(glsend.at[r, other_rows], glsib.at[r], sib_s.at[r], sib_r.at[r], sibling)

    def glz_copy(r):
        return remote(glz.at[r], glzr.at[z], glz_s.at[r], glz_r.at[z], at_z(z_at(r)))

    def chip_sum(r):
        sib_copy(r).wait_recv()
        return glsend[r, own_rows, :].astype(F32) + glsib[r].astype(F32)

    def second_pass(step, carry):
        r = nz - 1 - step
        rows = pl.ds(pl.multiple_of(r * tok, tok), tok)
        key_parts, value_parts, rope_parts = [], [], []
        for h in range(2):
            factor = jnp.exp2(mscr[h, r] - carry[h])
            probs = (pexp[h, r] * factor).astype(BF16)
            dscores = (dsx[h, r] * (factor * score_scale)).astype(BF16)
            dsall[h, rows, :] = dscores
            joint = dot(dscores, qcat[h])
            key_parts.append(joint[:, :DN].astype(BF16))
            rope_parts.append(joint[:, DN:])
            value_parts.append(dot(probs, qgo[h]).astype(BF16))
        grads = jnp.concatenate(key_parts + value_parts, axis=1)
        gall[rows, :] = grads
        ropes = jnp.where(
            lax.broadcasted_iota(jnp.int32, (tok, 2 * DR), 1) < DR, rope_parts[0], rope_parts[1]
        )
        glsend[r, :, 0:DL] = dot_nt(grads, w[...]).astype(BF16)
        glsend[r, :, DL:] = ropes.astype(BF16)
        sib_copy(r).start()

        @pl.when(step > 0)
        def _():
            glz[r + 1] = chip_sum(r + 1).astype(BF16)
            glz_copy(r + 1).start()

        return carry

    lax.fori_loop(0, nz, second_pass, tuple(log_total))

    parts = [dot(keyst[h], dsall[h]) for h in range(2)]
    stacked = jnp.concatenate(
        [parts[0][:DN], parts[1][:DN], parts[0][DN:] + parts[1][DN:]], axis=0
    )
    turned = stacked.T
    gqb[...] = turned.astype(BF16).reshape(gqb.shape)
    gqf[...] = turned
    gq_copies = [
        remote(gqb.at[p], gqr.at[x], gq_s.at[k], gq_r.at[x], at_x(p))
        for k, p in enumerate(x_peers)
    ]
    for copy in gq_copies:
        copy.start()

    sub = DL // (nz * NX)
    gwf[...] = dot(latt[...], gall[...]).reshape(gwf.shape)
    for p in range(NX):
        gwb[p] = gwf[:, p].astype(BF16)
    gwx_copies = [
        remote(gwb.at[p], gwr.at[x], gwx_s.at[k], gwx_r.at[x], at_x(p))
        for k, p in enumerate(x_peers)
    ]
    for copy in gwx_copies:
        copy.start()

    total = chip_sum(0)
    for k in range(1, nz):
        p = z_at(k)
        remote(glz.at[0], glzr.at[p], glz_s.at[0], glz_r.at[p], at_z(p)).wait_recv()
        total += glzr[p].astype(F32)
    tot[...] = total.reshape(tot.shape)
    ychunk[...] = total.astype(BF16).reshape(ychunk.shape)
    y_copies = [
        remote(ychunk.at[p], yrecv.at[y], y_s.at[k], y_r.at[y], at_head(p * CORES + core))
        for k, p in enumerate(y_peers)
    ]
    for copy in y_copies:
        copy.start()

    own_tok = pl.ds(pl.multiple_of(x * tok, tok), tok)
    mine = gqf[own_tok, :]
    for p in x_peers:
        remote(gqb.at[0], gqr.at[p], gq_s.at[0], gq_r.at[p], at_x(p)).wait_recv()
        mine += gqr[p].astype(F32)
    gqn_v[...] = mine[:, :2 * DN].astype(BF16)
    gqr_v[...] = mine[:, 2 * DN:].astype(BF16)
    out_copies = [
        pltpu.make_async_copy(gqn_v, gqn_out.at[0], out_sem.at[0]),
        pltpu.make_async_copy(gqr_v, gqr_out.at[0], out_sem.at[1]),
        pltpu.make_async_copy(gl_v, gl_out.at[0], out_sem.at[2]),
        pltpu.make_async_copy(gkr_v, gkr_out.at[0], out_sem.at[3]),
        pltpu.make_async_copy(gwk_v, gwk_out, out_sem.at[4]),
        pltpu.make_async_copy(gwv_v, gwv_out, out_sem.at[5]),
    ]
    for copy in out_copies[:2]:
        copy.start()

    part = gwf[:, x]
    for p in x_peers:
        remote(gwb.at[0], gwr.at[p], gwx_s.at[0], gwx_r.at[p], at_x(p)).wait_recv()
        part += gwr[p].astype(F32)
    gwzf[...] = part
    gwzb[...] = part.astype(BF16)
    gwz_copies = [
        remote(gwzb.at[z_at(r)], gwzr.at[z], gwz_s.at[r - 1], gwz_r.at[z], at_z(z_at(r)))
        for r in range(1, nz)
    ]
    for copy in gwz_copies:
        copy.start()

    mine = tot[y]
    for p in y_peers:
        remote(
            ychunk.at[0], yrecv.at[p], y_s.at[0], y_r.at[p], at_head(p * CORES + core)
        ).wait_recv()
        mine += yrecv[p].astype(F32)
    folded = mine[:, DL:] + jnp.concatenate([mine[:, DL + DR:], mine[:, DL:DL + DR]], axis=1)
    slot = core * nyh + y
    final[slot, :, 0:DL] = mine[:, :DL].astype(BF16)
    final[slot, :, DL:] = folded.astype(BF16)
    fin_copies = [
        remote(final.at[slot], final.at[slot], fin_s.at[k], fin_r.at[slot], at_head(p))
        for k, p in enumerate(head_peers)
    ]
    for copy in fin_copies:
        copy.start()

    part = gwzf[z]
    for r in range(1, nz):
        p = z_at(r)
        remote(gwzb.at[0], gwzr.at[p], gwz_s.at[0], gwz_r.at[p], at_z(p)).wait_recv()
        part += gwzr[p].astype(F32)
    gwdf[...] = part.reshape(gwdf.shape)
    dp_copy = remote(gwdf.at[1 - dp], gwdr, dp_s.at[0], dp_r.at[0], other_dp)
    dp_copy.start()

    for p in head_peers:
        from_slot = lax.rem(p, CORES) * nyh + lax.div(p, CORES)
        remote(
            final.at[from_slot], final.at[from_slot], fin_s.at[0], fin_r.at[from_slot], at_head(p)
        ).wait_recv()
    rows_16 = half // nyh
    for k in range(heads):
        gl_v[k * rows_16:(k + 1) * rows_16, :] = final[k, :, 0:DL]
    gkr_v[...] = jnp.concatenate([final[k, :, DL:] for k in range(heads)], axis=0).T[:DR]
    for copy in out_copies[2:4]:
        copy.start()

    dp_copy.wait_recv()
    summed = gwdf[dp] + gwdr[...]
    gwk_v[...] = summed[:, :2 * DN]
    gwv_v[...] = summed[:, 2 * DN:]
    for copy in out_copies[4:]:
        copy.start()

    for copy in (
        q_copies + lat_copies + delta_copies + stat_copies + gq_copies + gwx_copies + y_copies
        + gwz_copies + fin_copies + [dp_copy]
    ):
        copy.wait_send()

    def drain(r, carry):
        sib_copy(r).wait_send()

        @pl.when(r > 0)
        def _():
            forward_copy(z_at(r)).wait_send()
            glz_copy(r).wait_send()

        return carry

    lax.fori_loop(0, nz, drain, 0)
    for copy in out_copies:
        copy.wait()


def hand_over(*refs):
    count = len(refs) // 2
    for k in range(count):
        refs[count + k][...] = refs[k][...]


def solution(mesh):
    nz = mesh.shape["ctx"] // NX
    nyh = mesh.shape["head"] // CORES

    def shards(*args):
        tok = args[0].shape[1]
        half = tok // CORES
        queries, keys = NX * tok, nz * tok
        sub = DL // (nz * NX)
        rows_y = half // nyh
        wide = DL + 2 * DR
        q_wide = 2 * DN + 2 * DR + 2 * DV
        cols = 2 * DN + 2 * DV
        any_spec = pl.BlockSpec(memory_space=pl.ANY)
        vmem = pl.BlockSpec(memory_space=pltpu.VMEM)
        dma = pltpu.SemaphoreType.DMA
        heads = nyh * CORES
        scratch = [
            pltpu.VMEM((nz, tok, wide), BF16),
            pltpu.VMEM((DR, tok), BF16),
            pltpu.VMEM((NX, tok, q_wide), BF16),
            pltpu.VMEM((tok, 2 * DV), BF16),
            pltpu.VMEM((DL, cols), BF16),
            pltpu.VMEM((NX, 8, tok), F32),
            pltpu.VMEM((8, queries), jnp.int32),
            pltpu.VMEM((2, queries, DN + 2 * DR), BF16),
            pltpu.VMEM((2, queries, DV), BF16),
            pltpu.VMEM((DL, keys), BF16),
            pltpu.VMEM((2, DN + 2 * DR, keys), BF16),
            pltpu.VMEM((2, nz, tok, queries), F32),
            pltpu.VMEM((2, nz, tok, queries), F32),
            pltpu.VMEM((2, nz, 1, queries), F32),
            pltpu.VMEM((2, nz, 1, queries), F32),
            pltpu.VMEM((NX, 8, queries), F32),
            pltpu.VMEM((2, keys, queries), BF16),
            pltpu.VMEM((keys, cols), BF16),
            pltpu.VMEM((nz, tok, wide), BF16),
            pltpu.VMEM((nz, half, wide), BF16),
            pltpu.VMEM((nz, half, wide), BF16),
            pltpu.VMEM((nz, half, wide), BF16),
            pltpu.VMEM((nyh, rows_y, wide), F32),
            pltpu.VMEM((nyh, rows_y, wide), BF16),
            pltpu.VMEM((nyh, rows_y, wide), BF16),
            pltpu.VMEM((heads, rows_y, wide), BF16),
            pltpu.VMEM((queries, 2 * DN + 2 * DR), F32),
            pltpu.VMEM((NX, tok, 2 * DN + 2 * DR), BF16),
            pltpu.VMEM((NX, tok, 2 * DN + 2 * DR), BF16),
            pltpu.VMEM((nz, NX, sub, cols), F32),
            pltpu.VMEM((NX, nz, sub, cols), BF16),
            pltpu.VMEM((NX, nz, sub, cols), BF16),
            pltpu.VMEM((nz, sub, cols), F32),
            pltpu.VMEM((nz, sub, cols), BF16),
            pltpu.VMEM((nz, sub, cols), BF16),
            pltpu.VMEM((2, sub // 2, cols), F32),
            pltpu.VMEM((sub // 2, cols), F32),
            pltpu.VMEM((tok, 2 * DN), BF16),
            pltpu.VMEM((tok, 2 * DR), BF16),
            pltpu.VMEM((tok, DL), BF16),
            pltpu.VMEM((DR, tok), BF16),
            pltpu.VMEM((sub // 2, 2 * DN), F32),
            pltpu.VMEM((sub // 2, 2 * DV), F32),
            dma((8,)), dma((6,)),
            dma((nz,)), dma((nz,)), dma((nz,)), dma((nz,)),
            dma((NX,)), dma((NX,)), dma((NX,)), dma((NX,)), dma((NX,)), dma((NX,)),
            dma((nz,)), dma((nz,)), dma((nz,)), dma((nz,)),
            dma((NX,)), dma((NX,)), dma((NX,)), dma((NX,)), dma((nz,)), dma((nz,)),
            dma((nyh,)), dma((nyh,)), dma((heads,)), dma((heads,)), dma((1,)), dma((1,)),
        ]
        out_shape = (
            jax.ShapeDtypeStruct((1, tok, 2 * DN), BF16),
            jax.ShapeDtypeStruct((1, tok, 2 * DR), BF16),
            jax.ShapeDtypeStruct((1, tok, DL), BF16),
            jax.ShapeDtypeStruct((1, DR, tok), BF16),
            jax.ShapeDtypeStruct((sub // 2, 2 * DN), F32),
            jax.ShapeDtypeStruct((sub // 2, 2 * DV), F32),
        )
        results = pl.pallas_call(
            functools.partial(kernel, nz, nyh, tok),
            out_shape=out_shape,
            in_specs=[any_spec] * 8 + [pl.BlockSpec(memory_space=pltpu.SMEM)],
            out_specs=(any_spec,) * 6,
            scratch_shapes=scratch,
            compiler_params=pltpu.CompilerParams(
                collective_id=0, has_side_effects=True, vmem_limit_bytes=56 * 1024 * 1024
            ),
        )(args[0], jnp.swapaxes(args[1], 1, 2), *args[2:])
        results = pl.pallas_call(
            hand_over,
            out_shape=out_shape,
            in_specs=[vmem] * 6,
            out_specs=(vmem,) * 6,
        )(*results)
        return (*results[:3], jnp.swapaxes(results[3], 1, 2), *results[4:])

    return jax.shard_map(
        shards,
        mesh=mesh,
        in_specs=(
            P("dp", "ctx", None),
            P("dp", "ctx", None),
            P("dp", "ctx", "head"),
            P("dp", "ctx", "head"),
            P("dp", "ctx", "head"),
            P("dp", "ctx", "head"),
            P(None, "head"),
            P(None, "head"),
            P(),
        ),
        out_specs=(
            P("dp", "ctx", "head"),
            P("dp", "ctx", "head"),
            P("dp", "ctx", None),
            P("dp", "ctx", None),
            P(("ctx", "dp"), "head"),
            P(("ctx", "dp"), "head"),
        ),
        check_vma=False,
    )
```

```python
import functools
import math

import jax
import jax.numpy as jnp
from jax import lax
from jax.experimental import pallas as pl
from jax.experimental.pallas import tpu as pltpu
from jax.sharding import PartitionSpec as P

DL = 512
DN = 128
DR = 64
DV = 128
NX = 4
CORES = 2
HALF_GROUP = 64
LAT_SUBS = 4
SUBS = 2

QW = 2 * DN + 2 * DR + 2 * DV
KW = DN + 2 * DR
CW = 2 * DN + 2 * DV
LW = DL + 2 * DR
GW = 2 * DN + 2 * DR

MESH = pl.DeviceIdType.MESH
MASKED = -1.5e38
FLOOR = -1.0e38
F32 = jnp.float32
BF16 = jnp.bfloat16

NT = (((1,), (1,)), ((), ()))


def dot(a, b):
    return jnp.dot(a, b, preferred_element_type=F32)


def dot_nt(a, b):
    return lax.dot_general(a, b, NT, preferred_element_type=F32)


def kernel(
    nz, nyh, tok,
    lat_in, kr_in, qn_in, qr_in, go_in, so_in, wk_in, wv_in, order,
    gqn_out, gqr_out, gl_out, gkr_out, gwk_out, gwv_out,
    lat, krs, q, saved, w, qpos, qcat, qgo, latt, kcat, vals, keyst,
    pexp, dprob, mscr, lscr, stats, dsall, gall,
    glb, rsend, rrecv, tot, hsend, hsib, ybuf, final,
    gqf, gqsend, gqsib, gqb, gqr, gwf, gwsend, gwsib, gwb, gwr, gwzf, gwzb, gwzr, gwdf, gwdr,
    gqn_v, gqr_v, gl_v, gkr_v, gwk_v, gwv_v,
    local_sem, out_sem, lat_s, lat_r, q_s, q_r, w_s, w_r, st_s, st_r,
    rs_s, rs_r, gqs_s, gqs_r, gws_s, gws_r, gq_s, gq_r, gwx_s, gwx_r, gwz_s, gwz_r,
    half_s, half_r, y_s, y_r, fin_s, fin_r, dp_s, dp_r,
):
    ctx = lax.axis_index("ctx")
    head = lax.axis_index("head")
    dp = lax.axis_index("dp")
    z, x = lax.div(ctx, NX), lax.rem(ctx, NX)
    y, core = lax.div(head, CORES), lax.rem(head, CORES)
    queries = NX * tok
    blocks = nz // 2
    piece = tok // SUBS
    lat_piece = tok // LAT_SUBS
    half = tok // CORES
    score_scale = (DN + DR) ** -0.5
    log2_scale = score_scale * math.log2(math.e)
    sib_head = y * CORES + (1 - core)
    sib = 1 - core

    def at_z(peer):
        return {"ctx": peer * NX + x, "head": head, "dp": dp}

    def at_x(peer, head_index):
        return {"ctx": z * NX + peer, "head": head_index, "dp": dp}

    def at_head(peer):
        return {"ctx": ctx, "head": peer, "dp": dp}

    sibling = at_head(sib_head)
    other_dp = {"ctx": ctx, "head": head, "dp": 1 - dp}

    def remote(src, dst, send, recv, device):
        return pltpu.make_async_remote_copy(
            src_ref=src, dst_ref=dst, send_sem=send, recv_sem=recv,
            device_id=device, device_id_type=MESH,
        )

    def near(i, n):
        return [lax.rem(i + 1, n), lax.rem(i + n - 1, n)] if n > 2 else [1 - i]

    def others(i, n):
        return near(i, n) + [lax.rem(i + k, n) for k in range(2, n - 1)]

    z_peers, x_peers = others(z, nz), others(x, NX)
    x_near, y_near = near(x, NX), near(y, nyh)
    gather_to = at_z(lax.rem(z + (1 - core) * (nz - 1) + core, nz))
    sums_to = at_z(lax.rem(z + (1 - core) + core * (nz - 1), nz))
    y_devices = [at_head(p * CORES + core) for p in y_near]

    local = [
        pltpu.make_async_copy(lat_in.at[0], lat.at[0, :, pl.ds(0, DL)], local_sem.at[0]),
        pltpu.make_async_copy(kr_in.at[0], krs, local_sem.at[1]),
        pltpu.make_async_copy(qn_in.at[0], q.at[core, x, :, pl.ds(0, 2 * DN)], local_sem.at[2]),
        pltpu.make_async_copy(
            qr_in.at[0], q.at[core, x, :, pl.ds(2 * DN, 2 * DR)], local_sem.at[3]
        ),
        pltpu.make_async_copy(
            go_in.at[0], q.at[core, x, :, pl.ds(GW, 2 * DV)], local_sem.at[4]
        ),
        pltpu.make_async_copy(wk_in, w.at[core, :, pl.ds(0, 2 * DN)], local_sem.at[5]),
        pltpu.make_async_copy(wv_in, w.at[core, :, pl.ds(2 * DN, 2 * DV)], local_sem.at[6]),
        pltpu.make_async_copy(so_in.at[0], saved, local_sem.at[7]),
    ]
    for copy in local:
        copy.start()

    barrier = pltpu.get_barrier_semaphore()
    targets = (
        [at_z(p) for p in near(z, nz)] + [at_x(p, head) for p in x_near]
        + [sibling, other_dp] + y_devices
    )
    for target in targets:
        pl.semaphore_signal(barrier, inc=1, device_id=target, device_id_type=MESH)
    for copy in local:
        copy.wait()
    lat[0, :, DL:] = jnp.concatenate([krs[...].T, jnp.zeros((tok, DR), BF16)], axis=1)
    pl.semaphore_wait(barrier, len(targets))

    def lat_copy(m, j):
        rows = pl.ds(j * lat_piece, lat_piece)
        return remote(
            lat.at[m, rows], lat.at[m + 1, rows], lat_s.at[m * LAT_SUBS + j],
            lat_r.at[(m + 1) * LAT_SUBS + j], gather_to,
        )

    def q_copy(p, j, send, device, c=core):
        rows = pl.ds(j * half, half)
        return remote(
            q.at[c, p, rows], q.at[c, p, rows], q_s.at[send], q_r.at[(c * NX + p) * 2 + j], device
        )

    sent = []

    def start(copy):
        copy.start()
        sent.append(copy)

    for j in range(LAT_SUBS):
        start(lat_copy(0, j))
    for j in range(2):
        for k, p in enumerate(x_near):
            start(q_copy(x, (j + k) % 2, 2 * k + j, at_x(p, head)))
    start(remote(w.at[core], w.at[core], w_s.at[0], w_r.at[0], sibling))
    for j in range(2):
        start(q_copy(x, j, 4 + j, sibling))

    product = (q[core, x, :, GW:].astype(F32) * saved[...].astype(F32)).T
    stats[core, x, 0:1, queries // 2:] = jnp.sum(product[:DV], axis=0, keepdims=True)
    stats[core, x, 1:2, queries // 2:] = jnp.sum(product[DV:], axis=0, keepdims=True)

    lane = lax.broadcasted_iota(jnp.int32, (1, tok), 1)
    for p in range(NX):
        first = 2 * (z * NX + p)
        qpos[0:1, p * tok:(p + 1) * tok] = jnp.where(
            lane < HALF_GROUP,
            order[first] * HALF_GROUP + lane,
            order[first + 1] * HALF_GROUP + lane - HALF_GROUP,
        )

    def pass_on(m):
        def take():
            for j in range(LAT_SUBS):
                lat_copy(m - 1, j).wait_recv()
                if m < blocks - 1:
                    start(lat_copy(m, j))
                elif m == blocks - 1:
                    @pl.when(core == 1)
                    def _():
                        lat_copy(m, j).start()

        if m < blocks:
            take()
        else:
            pl.when(core == 1)(take)

    def project(s):
        slot = s + core
        latents = lat[slot, :, 0:DL]
        rope = lat[slot, :, DL:]
        ropes = (rope, jnp.concatenate([rope[:, DR:], rope[:, :DR]], axis=1))
        columns = slice(s * tok, (s + 1) * tok)
        latt[:, columns] = latents.T
        for c in range(CORES):
            projected = dot(latents, w[c]).astype(BF16)
            for h in range(2):
                hh = 2 * c + h
                key = jnp.concatenate([projected[:, h * DN:(h + 1) * DN], ropes[h]], axis=1)
                kcat[hh, columns, :] = key
                keyst[hh, :, columns] = key.T
                vals[hh, columns, :] = projected[:, 2 * DN + h * DV:2 * DN + (h + 1) * DV]

    def q_take(p, j, number, onward=None):
        q_copy(p, j, 0, sibling).wait_recv()
        if onward is not None:
            start(q_copy(p, j, 6 + j, at_x(onward, head)))
        start(q_copy(p, j, 8 + number, sibling))

    def q_first():
        if len(x_near) == 2:
            right, left = x_near
            q_take(left, 0, 0, right)
            q_take(right, 1, 1, left)

    def q_second():
        if len(x_near) == 2:
            right, left = x_near
            q_take(left, 1, 2)
            q_take(right, 0, 3)
        else:
            for j in range(2):
                q_take(x_near[0], j, j)

    def q_third():
        for p in x_peers[2:]:
            for j in range(2):
                q_take(p, j, 4 + j)

    pass_on(1)
    remote(w.at[sib], w.at[sib], w_s.at[0], w_r.at[0], sibling).wait_recv()
    q_first()
    project(0)
    for s in range(1, max(blocks, 4)):
        if s == 3:
            q_third()
        if s < blocks:
            pass_on(s + 1)
        if s == 1:
            q_second()
        if s < blocks:
            project(s)
    for p in range(NX):
        for j in range(2):
            q_copy(p, j, 0, sibling, sib).wait_recv()
    for p in range(NX):
        rows = slice(p * tok, (p + 1) * tok)
        for c in range(CORES):
            for h in range(2):
                qcat[2 * c + h, rows, 0:DN] = q[c, p, :, h * DN:(h + 1) * DN]
                qcat[2 * c + h, rows, DN:] = q[c, p, :, 2 * DN:GW]
                qgo[2 * c + h, rows, :] = q[c, p, :, GW + h * DV:GW + (h + 1) * DV]

    def first_pass(s, carry):
        slot = s + core
        block = lax.rem(z + (1 - core) * slot + core * (nz - slot), nz)
        first = 2 * (block * NX + x)
        rows = pl.ds(pl.multiple_of(s * tok, tok), tok)
        row = lax.broadcasted_iota(jnp.int32, (HALF_GROUP, queries), 0)
        where_q = qpos[0:1, :]
        seen = jnp.concatenate(
            [row <= where_q - order[first + g] * HALF_GROUP for g in range(2)], axis=0
        )
        for hh in range(2 * CORES):
            scores = jnp.where(seen, dot_nt(kcat[hh, rows, :], qcat[hh]) * log2_scale, MASKED)
            top = jnp.maximum(jnp.max(scores, axis=0, keepdims=True), FLOOR)
            weight = jnp.exp2(scores - top)
            mscr[hh, s] = top
            lscr[hh, s] = jnp.sum(weight, axis=0, keepdims=True)
            pexp[hh, s] = weight
            dprob[hh, s] = dot_nt(vals[hh, rows, :], qgo[hh])
        return carry

    lax.fori_loop(0, blocks, first_pass, 0)

    for hh in range(2 * CORES):
        top = mscr[hh, 0]
        for s in range(1, blocks):
            top = jnp.maximum(top, mscr[hh, s])
        total = jnp.zeros_like(top)
        for s in range(blocks):
            total += lscr[hh, s] * jnp.exp2(mscr[hh, s] - top)
        summary = top + jnp.log2(jnp.maximum(total, 1e-37))
        stats[core, x, 2 * hh:2 * hh + 1, 0:queries // 2] = summary[:, :queries // 2]
        stats[core, x, 2 * hh + 1:2 * hh + 2, 0:queries // 2] = summary[:, queries // 2:]
    partners = [(core, p, at_x(p, head)) for p in x_peers]
    partners += [(sib, p, at_x(p, sib_head)) for p in x_peers] + [(sib, x, sibling)]
    mine = core * NX + x
    for k, (_, _, device) in enumerate(partners):
        start(remote(stats.at[core, x], stats.at[core, x], st_s.at[k], st_r.at[mine], device))
    for c, p, device in partners:
        remote(
            stats.at[c, p], stats.at[c, p], st_s.at[0], st_r.at[c * NX + p], device
        ).wait_recv()
    log_total, row_delta = [], []
    everyone = [(c, p) for c in range(CORES) for p in range(NX)]
    for hh in range(2 * CORES):
        sums = [
            jnp.concatenate(
                [stats[c, p, 2 * hh + k:2 * hh + k + 1, 0:queries // 2] for k in range(2)], axis=1
            )
            for c, p in everyone
        ]
        top = functools.reduce(jnp.maximum, sums)
        total = functools.reduce(jnp.add, [jnp.exp2(one - top) for one in sums])
        log_total.append(top + jnp.log2(total))
        row_delta.append(jnp.concatenate(
            [stats[hh // 2, p, hh % 2:hh % 2 + 1, queries // 2:] for p in range(NX)], axis=1
        ))

    def block_sums(t):
        s = blocks - 1 - t
        rows = slice(s * tok, (s + 1) * tok)
        ropes = []
        latent_sum = None
        for c in range(CORES):
            key_parts, value_parts = [], []
            for hh in (2 * c, 2 * c + 1):
                factor = jnp.exp2(mscr[hh, s] - log_total[hh])
                probs = pexp[hh, s] * factor
                dscores = (probs * ((dprob[hh, s] - row_delta[hh]) * score_scale)).astype(BF16)
                dsall[hh, rows, :] = dscores
                joint = dot(dscores, qcat[hh])
                key_parts.append(joint[:, :DN].astype(BF16))
                ropes.append(joint[:, DN:])
                value_parts.append(dot(probs.astype(BF16), qgo[hh]).astype(BF16))
            grads = jnp.concatenate(key_parts + value_parts, axis=1)
            gall[c, rows, :] = grads
            part = dot_nt(grads, w[c])
            latent_sum = part if latent_sum is None else latent_sum + part
        glb[t, :, 0:DL] = latent_sum
        glb[t, :, DL:] = jnp.where(
            lax.broadcasted_iota(jnp.int32, (tok, 2 * DR), 1) < DR,
            ropes[0] + ropes[2], ropes[1] + ropes[3],
        )

    def ring_copy(t, j):
        rows = pl.ds(j * piece, piece)
        return remote(
            rsend.at[t, rows], rrecv.at[t, rows], rs_s.at[t * SUBS + j], rs_r.at[t * SUBS + j],
            sums_to,
        )

    def ring_step(t):
        for j in range(SUBS):
            rows = slice(j * piece, (j + 1) * piece)
            so_far = glb[t, rows, :]
            if t > 0:
                ring_copy(t - 1, j).wait_recv()
                so_far = so_far + rrecv[t - 1, rows, :].astype(F32)
            rsend[t, rows, :] = so_far.astype(BF16)
            if t < blocks - 1:
                start(ring_copy(t, j))
            else:
                tot[rows, :] = so_far

                @pl.when(core == 1)
                def _():
                    ring_copy(t, j).start()

        if t == blocks - 1:
            @pl.when(core == 0)
            def _():
                hsend[...] = tot[half:, :].astype(BF16)
                half_copy(hsend).start()

    def half_copy(source):
        return remote(source, hsib, half_s.at[0], half_r.at[0], sibling)

    def query_grads(c):
        parts = [dot(keyst[2 * c + h], dsall[2 * c + h]) for h in range(2)]
        return jnp.concatenate(
            [parts[0][:DN], parts[1][:DN], parts[0][DN:] + parts[1][DN:]], axis=0
        ).T

    gq_pass = remote(gqsend, gqsib, gqs_s.at[0], gqs_r.at[0], sibling)
    gw_pass = remote(gwsend, gwsib, gws_s.at[0], gws_r.at[0], sibling)

    def sibling_query_grads():
        gqsend[...] = query_grads(sib).astype(BF16).reshape(gqsend.shape)
        start(gq_pass)

    def sibling_weight_grads():
        gwsend[...] = dot(latt[...], gall[sib]).astype(BF16).reshape(gwsend.shape)
        start(gw_pass)

    def own_weight_grads():
        gwf[...] = dot(latt[...], gall[core]).reshape(gwf.shape)
        gw_pass.wait_recv()
        gwf[...] += gwsib[...].astype(F32)
        for p in range(NX):
            gwb[p] = gwf[:, p].astype(BF16)
        for k, p in enumerate(x_peers):
            start(remote(gwb.at[p], gwr.at[x], gwx_s.at[k], gwx_r.at[x], at_x(p, head)))

    def own_query_grads():
        own_queries = query_grads(core).reshape(gqf.shape)
        gq_pass.wait_recv()
        gqf[...] = own_queries + gqsib[...].astype(F32)
        gqb[...] = gqf[...].astype(BF16)
        for k, p in enumerate(x_peers):
            start(remote(gqb.at[p], gqr.at[x], gq_s.at[k], gq_r.at[x], at_x(p, head)))

    between = [[functools.partial(block_sums, t) for t in range(1, min(blocks, 3))]]
    between += [[functools.partial(block_sums, t)] for t in range(3, blocks)]
    while len(between) < 3:
        between.append([])
    between[1] += [sibling_weight_grads]
    between[2] += [sibling_query_grads, own_weight_grads]
    block_sums(0)
    ring_step(0)
    for t in range(1, blocks):
        for item in between.pop(0):
            item()
        ring_step(t)
    for item in sum(between, []):
        item()
    own_query_grads()

    own_rows = pl.ds(pl.multiple_of(core * half, half), half)

    @pl.when(core == 1)
    def _():
        for j in range(SUBS):
            ring_copy(blocks - 1, j).wait_recv()
            if j == SUBS // 2 - 1:
                half_copy(rrecv.at[blocks - 1, pl.ds(0, half)]).start()
        tot[half:, :] = rrecv[blocks - 1, half:, :].astype(F32)

    half_copy(hsend).wait_recv()
    ybuf[y] = (tot[own_rows, :] + hsib[...].astype(F32)).astype(BF16)

    yhalf = half // 2

    def y_copy(slot, j, send, device):
        rows = pl.ds(j * yhalf, yhalf)
        return remote(
            ybuf.at[slot, rows], ybuf.at[slot, rows], y_s.at[send], y_r.at[2 * slot + j], device
        )

    for j in range(2):
        for k, device in enumerate(y_devices):
            start(y_copy(y, (j + k) % 2, 2 * k + j, device))

    part = gwf[:, x]
    for p in x_peers:
        remote(gwb.at[0], gwr.at[p], gwx_s.at[0], gwx_r.at[p], at_x(p, head)).wait_recv()
        part += gwr[p].astype(F32)
    gwzf[...] = part
    gwzb[...] = part.astype(BF16)
    for k, p in enumerate(z_peers):
        start(remote(gwzb.at[p], gwzr.at[z], gwz_s.at[k], gwz_r.at[z], at_z(p)))

    if nyh > 2:
        right, left = y_near
        y_copy(left, 0, 0, sibling).wait_recv()
        start(y_copy(left, 0, 4, y_devices[0]))
        y_copy(right, 1, 0, sibling).wait_recv()
        start(y_copy(right, 1, 5, y_devices[1]))

    part = gqf[x]
    for p in x_peers:
        remote(gqb.at[0], gqr.at[p], gq_s.at[0], gq_r.at[p], at_x(p, head)).wait_recv()
        part += gqr[p].astype(F32)
    gqn_v[...] = part[:, :2 * DN].astype(BF16)
    gqr_v[...] = part[:, 2 * DN:].astype(BF16)
    out_copies = [
        pltpu.make_async_copy(gqn_v, gqn_out.at[0], out_sem.at[0]),
        pltpu.make_async_copy(gqr_v, gqr_out.at[0], out_sem.at[1]),
        pltpu.make_async_copy(gl_v, gl_out.at[0], out_sem.at[2]),
        pltpu.make_async_copy(gkr_v, gkr_out.at[0], out_sem.at[3]),
        pltpu.make_async_copy(gwk_v, gwk_out, out_sem.at[4]),
        pltpu.make_async_copy(gwv_v, gwv_out, out_sem.at[5]),
    ]
    for copy in out_copies[:2]:
        copy.start()

    part = gwzf[z]
    for p in z_peers:
        remote(gwzb.at[0], gwzr.at[p], gwz_s.at[0], gwz_r.at[p], at_z(p)).wait_recv()
        part += gwzr[p].astype(F32)
    gwdf[...] = part.reshape(gwdf.shape)
    dp_copy = remote(gwdf.at[1 - dp], gwdr, dp_s.at[0], dp_r.at[0], other_dp)
    start(dp_copy)

    if nyh > 2:
        y_copy(left, 1, 0, sibling).wait_recv()
        y_copy(right, 0, 0, sibling).wait_recv()
        far = others(y, nyh)[2]
        for j in range(2):
            y_copy(far, j, 0, sibling).wait_recv()
    else:
        for j in range(2):
            y_copy(y_near[0], j, 0, sibling).wait_recv()
    part = functools.reduce(jnp.add, [ybuf[k].astype(F32) for k in range(nyh)])
    folded = part[:, DL:] + jnp.concatenate([part[:, DL + DR:], part[:, DL:DL + DR]], axis=1)
    final[core, :, 0:DL] = part[:, :DL].astype(BF16)
    final[core, :, DL:] = folded.astype(BF16)
    start(remote(final.at[core], final.at[core], fin_s.at[0], fin_r.at[core], sibling))

    dp_copy.wait_recv()
    summed = gwdf[dp] + gwdr[...]
    gwk_v[...] = summed[:, :2 * DN]
    gwv_v[...] = summed[:, 2 * DN:]
    for copy in out_copies[4:]:
        copy.start()

    remote(final.at[sib], final.at[sib], fin_s.at[0], fin_r.at[sib], sibling).wait_recv()
    gl_v[...] = jnp.concatenate([final[c, :, 0:DL] for c in range(CORES)], axis=0)
    gkr_v[...] = jnp.concatenate([final[c, :, DL:] for c in range(CORES)], axis=0).T[:DR]
    for copy in out_copies[2:4]:
        copy.start()

    for copy in sent:
        copy.wait_send()
    half_copy(hsend).wait_send()

    @pl.when(core == 1)
    def _():
        for j in range(LAT_SUBS):
            lat_copy(blocks - 1, j).wait_send()
        for j in range(SUBS):
            ring_copy(blocks - 1, j).wait_send()

    for copy in out_copies:
        copy.wait()


def hand_over(*refs):
    count = len(refs) // 2
    for k in range(count):
        refs[count + k][...] = refs[k][...]


def solution(mesh):
    nz = mesh.shape["ctx"] // NX
    nyh = mesh.shape["head"] // CORES

    def shards(*args):
        tok = args[0].shape[1]
        queries = NX * tok
        blocks = nz // 2
        keys = blocks * tok
        sub = DL // (nz * NX)
        any_spec = pl.BlockSpec(memory_space=pl.ANY)
        vmem = pl.BlockSpec(memory_space=pltpu.VMEM)
        dma = pltpu.SemaphoreType.DMA
        scratch = [
            pltpu.VMEM((blocks + 1, tok, LW), BF16),
            pltpu.VMEM((DR, tok), BF16),
            pltpu.VMEM((CORES, NX, tok, QW), BF16),
            pltpu.VMEM((tok, 2 * DV), BF16),
            pltpu.VMEM((CORES, DL, CW), BF16),
            pltpu.VMEM((8, queries), jnp.int32),
            pltpu.VMEM((4, queries, KW), BF16),
            pltpu.VMEM((4, queries, DV), BF16),
            pltpu.VMEM((DL, keys), BF16),
            pltpu.VMEM((4, keys, KW), BF16),
            pltpu.VMEM((4, keys, DV), BF16),
            pltpu.VMEM((4, KW, keys), BF16),
            pltpu.VMEM((4, blocks, tok, queries), F32),
            pltpu.VMEM((4, blocks, tok, queries), F32),
            pltpu.VMEM((4, blocks, 1, queries), F32),
            pltpu.VMEM((4, blocks, 1, queries), F32),
            pltpu.VMEM((CORES, NX, 8, queries // 2 + tok), F32),
            pltpu.VMEM((4, keys, queries), BF16),
            pltpu.VMEM((CORES, keys, CW), BF16),
            pltpu.VMEM((blocks, tok, LW), F32),
            pltpu.VMEM((blocks, tok, LW), BF16),
            pltpu.VMEM((blocks, tok, LW), BF16),
            pltpu.VMEM((tok, LW), F32),
            pltpu.VMEM((tok // CORES, LW), BF16),
            pltpu.VMEM((tok // CORES, LW), BF16),
            pltpu.VMEM((nyh, tok // CORES, LW), BF16),
            pltpu.VMEM((CORES, tok // CORES, LW), BF16),
            pltpu.VMEM((NX, tok, GW), F32),
            pltpu.VMEM((NX, tok, GW), BF16),
            pltpu.VMEM((NX, tok, GW), BF16),
            pltpu.VMEM((NX, tok, GW), BF16),
            pltpu.VMEM((NX, tok, GW), BF16),
            pltpu.VMEM((nz, NX, sub, CW), F32),
            pltpu.VMEM((nz, NX, sub, CW), BF16),
            pltpu.VMEM((nz, NX, sub, CW), BF16),
            pltpu.VMEM((NX, nz, sub, CW), BF16),
            pltpu.VMEM((NX, nz, sub, CW), BF16),
            pltpu.VMEM((nz, sub, CW), F32),
            pltpu.VMEM((nz, sub, CW), BF16),
            pltpu.VMEM((nz, sub, CW), BF16),
            pltpu.VMEM((2, sub // 2, CW), F32),
            pltpu.VMEM((sub // 2, CW), F32),
            pltpu.VMEM((tok, 2 * DN), BF16),
            pltpu.VMEM((tok, 2 * DR), BF16),
            pltpu.VMEM((tok, DL), BF16),
            pltpu.VMEM((DR, tok), BF16),
            pltpu.VMEM((sub // 2, 2 * DN), F32),
            pltpu.VMEM((sub // 2, 2 * DV), F32),
            dma((8,)), dma((6,)),
            dma((LAT_SUBS * (blocks + 1),)), dma((LAT_SUBS * (blocks + 1),)),
            dma((14,)), dma((2 * CORES * NX,)), dma((1,)), dma((1,)),
            dma((CORES * NX,)), dma((CORES * NX,)),
            dma((SUBS * blocks,)), dma((SUBS * blocks,)),
            dma((1,)), dma((1,)), dma((1,)), dma((1,)),
            dma((NX,)), dma((NX,)), dma((NX,)), dma((NX,)), dma((nz,)), dma((nz,)),
            dma((1,)), dma((1,)), dma((6,)), dma((2 * nyh,)),
            dma((1,)), dma((CORES,)), dma((1,)), dma((1,)),
        ]
        out_shape = (
            jax.ShapeDtypeStruct((1, tok, 2 * DN), BF16),
            jax.ShapeDtypeStruct((1, tok, 2 * DR), BF16),
            jax.ShapeDtypeStruct((1, tok, DL), BF16),
            jax.ShapeDtypeStruct((1, DR, tok), BF16),
            jax.ShapeDtypeStruct((sub // 2, 2 * DN), F32),
            jax.ShapeDtypeStruct((sub // 2, 2 * DV), F32),
        )
        results = pl.pallas_call(
            functools.partial(kernel, nz, nyh, tok),
            out_shape=out_shape,
            in_specs=[any_spec] * 8 + [pl.BlockSpec(memory_space=pltpu.SMEM)],
            out_specs=(any_spec,) * 6,
            scratch_shapes=scratch,
            compiler_params=pltpu.CompilerParams(
                collective_id=0, has_side_effects=True, vmem_limit_bytes=56 * 1024 * 1024
            ),
        )(args[0], jnp.swapaxes(args[1], 1, 2), *args[2:])
        results = pl.pallas_call(
            hand_over,
            out_shape=out_shape,
            in_specs=[vmem] * 6,
            out_specs=(vmem,) * 6,
        )(*results)
        return (*results[:3], jnp.swapaxes(results[3], 1, 2), *results[4:])

    return jax.shard_map(
        shards,
        mesh=mesh,
        in_specs=(
            P("dp", "ctx", None),
            P("dp", "ctx", None),
            P("dp", "ctx", "head"),
            P("dp", "ctx", "head"),
            P("dp", "ctx", "head"),
            P("dp", "ctx", "head"),
            P(None, "head"),
            P(None, "head"),
            P(),
        ),
        out_specs=(
            P("dp", "ctx", "head"),
            P("dp", "ctx", "head"),
            P("dp", "ctx", None),
            P("dp", "ctx", None),
            P(("ctx", "dp"), "head"),
            P(("ctx", "dp"), "head"),
        ),
        check_vma=False,
    )
```

```python
import functools
import math

import jax
import jax.numpy as jnp
from jax import lax
from jax.experimental import pallas as pl
from jax.experimental.pallas import tpu as pltpu
from jax.sharding import PartitionSpec as P

DL = 512
DN = 128
DR = 64
DV = 128
NX = 4
CORES = 2
HALF_GROUP = 64
LAT_SUBS = 4
SUBS = 4

QW = 2 * DN + 2 * DR + 2 * DV
KW = DN + 2 * DR
CW = 2 * DN + 2 * DV
LW = DL + 2 * DR
GW = 2 * DN + 2 * DR

MESH = pl.DeviceIdType.MESH
MASKED = -1.5e38
FLOOR = -1.0e38
F32 = jnp.float32
BF16 = jnp.bfloat16

NT = (((1,), (1,)), ((), ()))


def dot(a, b):
    return jnp.dot(a, b, preferred_element_type=F32)


def dot_nt(a, b):
    return lax.dot_general(a, b, NT, preferred_element_type=F32)


def kernel(
    nz, nyh, tok,
    lat_in, kr_in, qn_in, qr_in, go_in, so_in, wk_in, wv_in, order,
    gqn_out, gqr_out, gl_out, gkr_out, gwk_out, gwv_out,
    lat, krs, q, saved, w, qpos, qcat, qgo, latt, kcat, vals, keyst,
    pexp, dprob, mscr, lscr, stats, dsall, gall,
    glb, rsend, rrecv, tot, hsend, hsib, ybuf, final,
    gqf, gqsend, gqsib, gqb, gqr, gqfar, gwf, gwsend, gwsib, gwb, gwr, gwfar, gwzf, gwzb, gwzr, gwdf, gwdr,
    gqn_v, gqr_v, gl_v, gkr_v, gwk_v, gwv_v,
    local_sem, out_sem, lat_s, lat_r, q_s, q_r, w_s, w_r, st_s, st_r,
    rs_s, rs_r, gqs_s, gqs_r, gws_s, gws_r, gq_s, gq_r, gwx_s, gwx_r, gwz_s, gwz_r,
    half_s, half_r, y_s, y_r, fin_s, fin_r, dp_s, dp_r,
):
    ctx = lax.axis_index("ctx")
    head = lax.axis_index("head")
    dp = lax.axis_index("dp")
    z, x = lax.div(ctx, NX), lax.rem(ctx, NX)
    y, core = lax.div(head, CORES), lax.rem(head, CORES)
    queries = NX * tok
    blocks = nz // 2
    piece = tok // SUBS
    lat_piece = tok // LAT_SUBS
    half = tok // CORES
    score_scale = (DN + DR) ** -0.5
    log2_scale = score_scale * math.log2(math.e)
    sib_head = y * CORES + (1 - core)
    sib = 1 - core

    def at_z(peer):
        return {"ctx": peer * NX + x, "head": head, "dp": dp}

    def at_x(peer, head_index):
        return {"ctx": z * NX + peer, "head": head_index, "dp": dp}

    def at_head(peer):
        return {"ctx": ctx, "head": peer, "dp": dp}

    sibling = at_head(sib_head)
    other_dp = {"ctx": ctx, "head": head, "dp": 1 - dp}

    def remote(src, dst, send, recv, device):
        return pltpu.make_async_remote_copy(
            src_ref=src, dst_ref=dst, send_sem=send, recv_sem=recv,
            device_id=device, device_id_type=MESH,
        )

    def near(i, n):
        return [lax.rem(i + 1, n), lax.rem(i + n - 1, n)] if n > 2 else [1 - i]

    def others(i, n):
        return near(i, n) + [lax.rem(i + k, n) for k in range(2, n - 1)]

    z_peers, x_peers = others(z, nz), others(x, NX)
    x_near, y_near = near(x, NX), near(y, nyh)
    gather_to = at_z(lax.rem(z + (1 - core) * (nz - 1) + core, nz))
    sums_to = at_z(lax.rem(z + (1 - core) + core * (nz - 1), nz))
    y_devices = [at_head(p * CORES + core) for p in y_near]

    local = [
        pltpu.make_async_copy(lat_in.at[0], lat.at[0, :, pl.ds(0, DL)], local_sem.at[0]),
        pltpu.make_async_copy(kr_in.at[0], krs, local_sem.at[1]),
        pltpu.make_async_copy(qn_in.at[0], q.at[core, x, :, pl.ds(0, 2 * DN)], local_sem.at[2]),
        pltpu.make_async_copy(
            qr_in.at[0], q.at[core, x, :, pl.ds(2 * DN, 2 * DR)], local_sem.at[3]
        ),
        pltpu.make_async_copy(
            go_in.at[0], q.at[core, x, :, pl.ds(GW, 2 * DV)], local_sem.at[4]
        ),
        pltpu.make_async_copy(wk_in, w.at[core, :, pl.ds(0, 2 * DN)], local_sem.at[5]),
        pltpu.make_async_copy(wv_in, w.at[core, :, pl.ds(2 * DN, 2 * DV)], local_sem.at[6]),
        pltpu.make_async_copy(so_in.at[0], saved, local_sem.at[7]),
    ]
    barrier = pltpu.get_barrier_semaphore()
    targets = (
        [at_z(p) for p in near(z, nz)] + [at_x(p, head) for p in x_near]
        + [sibling, other_dp] + y_devices
    )
    for target in targets:
        pl.semaphore_signal(barrier, inc=1, device_id=target, device_id_type=MESH)
    for copy in local:
        copy.start()
    for copy in local[:2]:
        copy.wait()
    lat[0, :, DL:] = jnp.concatenate([krs[...].T, jnp.zeros((tok, DR), BF16)], axis=1)
    for copy in local[2:5]:
        copy.wait()
    pl.semaphore_wait(barrier, len(targets))

    def lat_copy(m, j):
        rows = pl.ds(j * lat_piece, lat_piece)
        return remote(
            lat.at[m, rows], lat.at[m + 1, rows], lat_s.at[m * LAT_SUBS + j],
            lat_r.at[(m + 1) * LAT_SUBS + j], gather_to,
        )

    def q_copy(p, j, send, device, c=core):
        rows = pl.ds(j * half, half)
        return remote(
            q.at[c, p, rows], q.at[c, p, rows], q_s.at[send], q_r.at[(c * NX + p) * 2 + j], device
        )

    sent = []

    def start(copy):
        copy.start()
        sent.append(copy)

    for j in range(LAT_SUBS):
        start(lat_copy(0, j))
    for j in range(2):
        for k, p in enumerate(x_near):
            start(q_copy(x, (j + k) % 2, 2 * k + j, at_x(p, head)))
    for copy in local[5:]:
        copy.wait()
    start(remote(w.at[core], w.at[core], w_s.at[0], w_r.at[0], sibling))
    for j in range(2):
        start(q_copy(x, j, 4 + j, sibling))

    product = (q[core, x, :, GW:].astype(F32) * saved[...].astype(F32)).T
    stats[core, x, 0:1, queries // 2:] = jnp.sum(product[:DV], axis=0, keepdims=True)
    stats[core, x, 1:2, queries // 2:] = jnp.sum(product[DV:], axis=0, keepdims=True)

    lane = lax.broadcasted_iota(jnp.int32, (1, tok), 1)
    for p in range(NX):
        first = 2 * (z * NX + p)
        qpos[0:1, p * tok:(p + 1) * tok] = jnp.where(
            lane < HALF_GROUP,
            order[first] * HALF_GROUP + lane,
            order[first + 1] * HALF_GROUP + lane - HALF_GROUP,
        )

    def pass_on(m):
        def take():
            for j in range(LAT_SUBS):
                lat_copy(m - 1, j).wait_recv()
                if m < blocks - 1:
                    start(lat_copy(m, j))
                elif m == blocks - 1:
                    @pl.when(core == 1)
                    def _():
                        lat_copy(m, j).start()

        if m < blocks:
            take()
        else:
            pl.when(core == 1)(take)

    def project(s):
        slot = s + core
        latents = lat[slot, :, 0:DL]
        rope = lat[slot, :, DL:]
        ropes = (rope, jnp.concatenate([rope[:, DR:], rope[:, :DR]], axis=1))
        columns = slice(s * tok, (s + 1) * tok)
        latt[:, columns] = latents.T
        for c in range(CORES):
            projected = dot(latents, w[c]).astype(BF16)
            for h in range(2):
                hh = 2 * c + h
                key = jnp.concatenate([projected[:, h * DN:(h + 1) * DN], ropes[h]], axis=1)
                kcat[hh, columns, :] = key
                keyst[hh, :, columns] = key.T
                vals[hh, columns, :] = projected[:, 2 * DN + h * DV:2 * DN + (h + 1) * DV]

    def q_take(p, j, number, onward=None):
        q_copy(p, j, 0, sibling).wait_recv()
        if onward is not None:
            start(q_copy(p, j, 6 + j, at_x(onward, head)))
        start(q_copy(p, j, 8 + number, sibling))

    def q_first():
        if len(x_near) == 2:
            right, left = x_near
            q_take(left, 0, 0, right)
            q_take(right, 1, 1, left)

    def q_second():
        if len(x_near) == 2:
            right, left = x_near
            q_take(left, 1, 2)
            q_take(right, 0, 3)
        else:
            for j in range(2):
                q_take(x_near[0], j, j)

    def q_third():
        for p in x_peers[2:]:
            for j in range(2):
                q_take(p, j, 4 + j)

    pass_on(1)
    remote(w.at[sib], w.at[sib], w_s.at[0], w_r.at[0], sibling).wait_recv()
    q_first()
    project(0)
    for s in range(1, max(blocks, 4)):
        if s == 3:
            q_third()
        if s < blocks:
            pass_on(s + 1)
        if s == 1:
            q_second()
        if s < blocks:
            project(s)
    for p in range(NX):
        for j in range(2):
            q_copy(p, j, 0, sibling, sib).wait_recv()
    for p in range(NX):
        rows = slice(p * tok, (p + 1) * tok)
        for c in range(CORES):
            for h in range(2):
                qcat[2 * c + h, rows, 0:DN] = q[c, p, :, h * DN:(h + 1) * DN]
                qcat[2 * c + h, rows, DN:] = q[c, p, :, 2 * DN:GW]
                qgo[2 * c + h, rows, :] = q[c, p, :, GW + h * DV:GW + (h + 1) * DV]

    def first_pass(s, carry):
        slot = s + core
        block = lax.rem(z + (1 - core) * slot + core * (nz - slot), nz)
        first = 2 * (block * NX + x)
        rows = pl.ds(pl.multiple_of(s * tok, tok), tok)
        row = lax.broadcasted_iota(jnp.int32, (HALF_GROUP, queries), 0)
        where_q = qpos[0:1, :]
        seen = jnp.concatenate(
            [row <= where_q - order[first + g] * HALF_GROUP for g in range(2)], axis=0
        )
        for hh in range(2 * CORES):
            scores = jnp.where(seen, dot_nt(kcat[hh, rows, :], qcat[hh]) * log2_scale, MASKED)
            top = jnp.maximum(jnp.max(scores, axis=0, keepdims=True), FLOOR)
            weight = jnp.exp2(scores - top)
            mscr[hh, s] = top
            lscr[hh, s] = jnp.sum(weight, axis=0, keepdims=True)
            pexp[hh, s] = weight
        return carry

    lax.fori_loop(0, blocks, first_pass, 0)

    for hh in range(2 * CORES):
        top = mscr[hh, 0]
        for s in range(1, blocks):
            top = jnp.maximum(top, mscr[hh, s])
        total = jnp.zeros_like(top)
        for s in range(blocks):
            total += lscr[hh, s] * jnp.exp2(mscr[hh, s] - top)
        summary = top + jnp.log2(jnp.maximum(total, 1e-37))
        stats[core, x, 2 * hh:2 * hh + 1, 0:queries // 2] = summary[:, :queries // 2]
        stats[core, x, 2 * hh + 1:2 * hh + 2, 0:queries // 2] = summary[:, queries // 2:]
    partners = [(core, p, at_x(p, head)) for p in x_peers]
    partners += [(sib, p, at_x(p, sib_head)) for p in x_peers] + [(sib, x, sibling)]
    mine = core * NX + x
    for k, (_, _, device) in enumerate(partners):
        start(remote(stats.at[core, x], stats.at[core, x], st_s.at[k], st_r.at[mine], device))

    def cotangents(s, carry):
        rows = pl.ds(pl.multiple_of(s * tok, tok), tok)
        for hh in range(2 * CORES):
            dprob[hh, s] = dot_nt(vals[hh, rows, :], qgo[hh])
        return carry

    lax.fori_loop(0, blocks, cotangents, 0)
    for c, p, device in partners:
        remote(
            stats.at[c, p], stats.at[c, p], st_s.at[0], st_r.at[c * NX + p], device
        ).wait_recv()
    log_total, row_delta = [], []
    everyone = [(c, p) for c in range(CORES) for p in range(NX)]
    for hh in range(2 * CORES):
        sums = [
            jnp.concatenate(
                [stats[c, p, 2 * hh + k:2 * hh + k + 1, 0:queries // 2] for k in range(2)], axis=1
            )
            for c, p in everyone
        ]
        top = functools.reduce(jnp.maximum, sums)
        total = functools.reduce(jnp.add, [jnp.exp2(one - top) for one in sums])
        log_total.append(top + jnp.log2(total))
        row_delta.append(jnp.concatenate(
            [stats[hh // 2, p, hh % 2:hh % 2 + 1, queries // 2:] for p in range(NX)], axis=1
        ))

    def block_sums(t):
        s = blocks - 1 - t
        rows = slice(s * tok, (s + 1) * tok)
        ropes = []
        latent_sum = None
        for c in range(CORES):
            key_parts, value_parts = [], []
            for hh in (2 * c, 2 * c + 1):
                factor = jnp.exp2(mscr[hh, s] - log_total[hh])
                probs = pexp[hh, s] * factor
                dscores = (probs * ((dprob[hh, s] - row_delta[hh]) * score_scale)).astype(BF16)
                dsall[hh, rows, :] = dscores
                joint = dot(dscores, qcat[hh])
                key_parts.append(joint[:, :DN].astype(BF16))
                ropes.append(joint[:, DN:])
                value_parts.append(dot(probs.astype(BF16), qgo[hh]).astype(BF16))
            grads = jnp.concatenate(key_parts + value_parts, axis=1)
            gall[c, rows, :] = grads
            part = dot_nt(grads, w[c])
            latent_sum = part if latent_sum is None else latent_sum + part
        glb[t, :, 0:DL] = latent_sum
        glb[t, :, DL:] = jnp.where(
            lax.broadcasted_iota(jnp.int32, (tok, 2 * DR), 1) < DR,
            ropes[0] + ropes[2], ropes[1] + ropes[3],
        )

    def ring_copy(t, j):
        rows = pl.ds(j * piece, piece)
        return remote(
            rsend.at[t, rows], rrecv.at[t, rows], rs_s.at[t * SUBS + j], rs_r.at[t * SUBS + j],
            sums_to,
        )

    def ring_step(t):
        for j in range(SUBS):
            rows = slice(j * piece, (j + 1) * piece)
            so_far = glb[t, rows, :]
            if t > 0:
                ring_copy(t - 1, j).wait_recv()
                so_far = so_far + rrecv[t - 1, rows, :].astype(F32)
            rsend[t, rows, :] = so_far.astype(BF16)
            if t < blocks - 1:
                start(ring_copy(t, j))
            else:
                tot[rows, :] = so_far

                @pl.when(core == 1)
                def _():
                    ring_copy(t, j).start()

        if t == blocks - 1:
            @pl.when(core == 0)
            def _():
                hsend[...] = tot[half:, :].astype(BF16)
                half_copy(hsend).start()

    def half_copy(source):
        return remote(source, hsib, half_s.at[0], half_r.at[0], sibling)

    def query_grads(c):
        parts = [dot(keyst[2 * c + h], dsall[2 * c + h]) for h in range(2)]
        return jnp.concatenate(
            [parts[0][:DN], parts[1][:DN], parts[0][DN:] + parts[1][DN:]], axis=0
        ).T

    gq_pass = remote(gqsend, gqsib, gqs_s.at[0], gqs_r.at[0], sibling)
    gw_pass = remote(gwsend, gwsib, gws_s.at[0], gws_r.at[0], sibling)

    def sibling_query_grads():
        gqsend[...] = query_grads(sib).astype(BF16).reshape(gqsend.shape)
        start(gq_pass)

    def sibling_weight_grads():
        gwsend[...] = dot(latt[...], gall[sib]).astype(BF16).reshape(gwsend.shape)
        start(gw_pass)

    class Scatter:
        def __init__(self, blocks, arrived, far, send, recv):
            self.blocks, self.arrived, self.far = blocks, arrived, far
            self.send, self.recv = send, recv
            self.size = far.shape[1]

        def copy(self, src, dst, k, kind):
            return remote(
                src, dst, self.send.at[3 * k + kind], self.recv.at[3 * k + kind],
                at_x(x_near[k], head),
            )

        def part(self, ref, j):
            return ref.at[pl.ds(j * self.size, self.size)]

        def far_copy(self, k):
            return self.copy(
                self.part(self.blocks.at[lax.rem(x + 2, NX)], k), self.far.at[k], k, 0
            )

        def near_copy(self, k, kind):
            j = k if kind == 2 else 1 - k
            return self.copy(
                self.part(self.blocks.at[x_near[k]], j), self.part(self.arrived.at[k], j), k, kind
            )

        def begin(self):
            if len(x_near) == 2:
                for k in range(2):
                    start(self.far_copy(k))
            for k in range(len(x_near)):
                start(self.near_copy(k, 1))
                if len(x_near) == 1:
                    start(self.near_copy(k, 2))

        def pass_on(self):
            if len(x_near) == 2:
                for k in range(2):
                    self.far_copy(k).wait_recv()
                    rows = slice(k * self.size, (k + 1) * self.size)
                    p = x_near[k]
                    self.blocks[p, rows] = (
                        self.blocks[p, rows].astype(F32) + self.far[k].astype(F32)
                    ).astype(BF16)
                    start(self.near_copy(k, 2))

        def finish(self, own):
            for k in range(len(x_near)):
                for kind in (1, 2):
                    self.near_copy(k, kind).wait_recv()
                own += self.arrived[k].astype(F32)
            return own

    gw_scatter = Scatter(gwb, gwr, gwfar, gwx_s, gwx_r)
    gq_scatter = Scatter(gqb, gqr, gqfar, gq_s, gq_r)

    def own_weight_grads():
        gwf[...] = dot(latt[...], gall[core]).reshape(gwf.shape)
        gw_pass.wait_recv()
        gwf[...] += gwsib[...].astype(F32)
        for p in range(NX):
            gwb[p] = gwf[:, p].astype(BF16)
        gw_scatter.begin()

    def own_query_grads():
        own_queries = query_grads(core).reshape(gqf.shape)
        gq_pass.wait_recv()
        gqf[...] = own_queries + gqsib[...].astype(F32)
        gqb[...] = gqf[...].astype(BF16)

    between = [[functools.partial(block_sums, t) for t in range(1, min(blocks, 3))]]
    between += [[functools.partial(block_sums, t)] for t in range(3, blocks)]
    while len(between) < 3:
        between.append([])
    between[1] += [sibling_weight_grads]
    between[2] += [sibling_query_grads, own_weight_grads]
    block_sums(0)
    ring_step(0)
    for t in range(1, blocks):
        for item in between.pop(0):
            item()
        ring_step(t)
    for item in sum(between, []):
        item()
    own_query_grads()
    gw_scatter.pass_on()
    gq_scatter.begin()

    own_rows = pl.ds(pl.multiple_of(core * half, half), half)

    @pl.when(core == 1)
    def _():
        for j in range(SUBS):
            ring_copy(blocks - 1, j).wait_recv()
            if j == SUBS // 2 - 1:
                half_copy(rrecv.at[blocks - 1, pl.ds(0, half)]).start()
        tot[half:, :] = rrecv[blocks - 1, half:, :].astype(F32)

    half_copy(hsend).wait_recv()
    ybuf[y] = (tot[own_rows, :] + hsib[...].astype(F32)).astype(BF16)

    yhalf = half // 2

    def y_copy(slot, j, send, device):
        rows = pl.ds(j * yhalf, yhalf)
        return remote(
            ybuf.at[slot, rows], ybuf.at[slot, rows], y_s.at[send], y_r.at[2 * slot + j], device
        )

    for j in range(2):
        for k, device in enumerate(y_devices):
            start(y_copy(y, (j + k) % 2, 2 * k + j, device))

    part = gw_scatter.finish(gwf[:, x])
    gwzf[...] = part
    gwzb[...] = part.astype(BF16)
    for k, p in enumerate(z_peers):
        start(remote(gwzb.at[p], gwzr.at[z], gwz_s.at[k], gwz_r.at[z], at_z(p)))

    gq_scatter.pass_on()
    if nyh > 2:
        right, left = y_near
        y_copy(left, 0, 0, sibling).wait_recv()
        start(y_copy(left, 0, 4, y_devices[0]))
        y_copy(right, 1, 0, sibling).wait_recv()
        start(y_copy(right, 1, 5, y_devices[1]))

    part = gq_scatter.finish(gqf[x])
    gqn_v[...] = part[:, :2 * DN].astype(BF16)
    gqr_v[...] = part[:, 2 * DN:].astype(BF16)
    out_copies = [
        pltpu.make_async_copy(gqn_v, gqn_out.at[0], out_sem.at[0]),
        pltpu.make_async_copy(gqr_v, gqr_out.at[0], out_sem.at[1]),
        pltpu.make_async_copy(gl_v, gl_out.at[0], out_sem.at[2]),
        pltpu.make_async_copy(gkr_v, gkr_out.at[0], out_sem.at[3]),
        pltpu.make_async_copy(gwk_v, gwk_out, out_sem.at[4]),
        pltpu.make_async_copy(gwv_v, gwv_out, out_sem.at[5]),
    ]
    for copy in out_copies[:2]:
        copy.start()

    part = gwzf[z]
    for p in z_peers:
        remote(gwzb.at[0], gwzr.at[p], gwz_s.at[0], gwz_r.at[p], at_z(p)).wait_recv()
        part += gwzr[p].astype(F32)
    gwdf[...] = part.reshape(gwdf.shape)
    dp_copy = remote(gwdf.at[1 - dp], gwdr, dp_s.at[0], dp_r.at[0], other_dp)
    start(dp_copy)

    if nyh > 2:
        y_copy(left, 1, 0, sibling).wait_recv()
        y_copy(right, 0, 0, sibling).wait_recv()
        far = others(y, nyh)[2]
        for j in range(2):
            y_copy(far, j, 0, sibling).wait_recv()
    else:
        for j in range(2):
            y_copy(y_near[0], j, 0, sibling).wait_recv()
    part = functools.reduce(jnp.add, [ybuf[k].astype(F32) for k in range(nyh)])
    folded = part[:, DL:] + jnp.concatenate([part[:, DL + DR:], part[:, DL:DL + DR]], axis=1)
    final[core, :, 0:DL] = part[:, :DL].astype(BF16)
    final[core, :, DL:] = folded.astype(BF16)
    start(remote(final.at[core], final.at[core], fin_s.at[0], fin_r.at[core], sibling))

    dp_copy.wait_recv()
    summed = gwdf[dp] + gwdr[...]
    gwk_v[...] = summed[:, :2 * DN]
    gwv_v[...] = summed[:, 2 * DN:]
    for copy in out_copies[4:]:
        copy.start()

    remote(final.at[sib], final.at[sib], fin_s.at[0], fin_r.at[sib], sibling).wait_recv()
    gl_v[...] = jnp.concatenate([final[c, :, 0:DL] for c in range(CORES)], axis=0)
    gkr_v[...] = jnp.concatenate([final[c, :, DL:] for c in range(CORES)], axis=0).T[:DR]
    for copy in out_copies[2:4]:
        copy.start()

    for copy in sent:
        copy.wait_send()
    half_copy(hsend).wait_send()

    @pl.when(core == 1)
    def _():
        for j in range(LAT_SUBS):
            lat_copy(blocks - 1, j).wait_send()
        for j in range(SUBS):
            ring_copy(blocks - 1, j).wait_send()

    for copy in out_copies:
        copy.wait()


def hand_over(*refs):
    count = len(refs) // 2
    for k in range(count):
        refs[count + k][...] = refs[k][...]


def solution(mesh):
    nz = mesh.shape["ctx"] // NX
    nyh = mesh.shape["head"] // CORES

    def shards(*args):
        tok = args[0].shape[1]
        queries = NX * tok
        blocks = nz // 2
        keys = blocks * tok
        sub = DL // (nz * NX)
        any_spec = pl.BlockSpec(memory_space=pl.ANY)
        vmem = pl.BlockSpec(memory_space=pltpu.VMEM)
        dma = pltpu.SemaphoreType.DMA
        scratch = [
            pltpu.VMEM((blocks + 1, tok, LW), BF16),
            pltpu.VMEM((DR, tok), BF16),
            pltpu.VMEM((CORES, NX, tok, QW), BF16),
            pltpu.VMEM((tok, 2 * DV), BF16),
            pltpu.VMEM((CORES, DL, CW), BF16),
            pltpu.VMEM((8, queries), jnp.int32),
            pltpu.VMEM((4, queries, KW), BF16),
            pltpu.VMEM((4, queries, DV), BF16),
            pltpu.VMEM((DL, keys), BF16),
            pltpu.VMEM((4, keys, KW), BF16),
            pltpu.VMEM((4, keys, DV), BF16),
            pltpu.VMEM((4, KW, keys), BF16),
            pltpu.VMEM((4, blocks, tok, queries), F32),
            pltpu.VMEM((4, blocks, tok, queries), F32),
            pltpu.VMEM((4, blocks, 1, queries), F32),
            pltpu.VMEM((4, blocks, 1, queries), F32),
            pltpu.VMEM((CORES, NX, 8, queries // 2 + tok), F32),
            pltpu.VMEM((4, keys, queries), BF16),
            pltpu.VMEM((CORES, keys, CW), BF16),
            pltpu.VMEM((blocks, tok, LW), F32),
            pltpu.VMEM((blocks, tok, LW), BF16),
            pltpu.VMEM((blocks, tok, LW), BF16),
            pltpu.VMEM((tok, LW), F32),
            pltpu.VMEM((tok // CORES, LW), BF16),
            pltpu.VMEM((tok // CORES, LW), BF16),
            pltpu.VMEM((nyh, tok // CORES, LW), BF16),
            pltpu.VMEM((CORES, tok // CORES, LW), BF16),
            pltpu.VMEM((NX, tok, GW), F32),
            pltpu.VMEM((NX, tok, GW), BF16),
            pltpu.VMEM((NX, tok, GW), BF16),
            pltpu.VMEM((NX, tok, GW), BF16),
            pltpu.VMEM((2, tok, GW), BF16),
            pltpu.VMEM((2, tok // 2, GW), BF16),
            pltpu.VMEM((nz, NX, sub, CW), F32),
            pltpu.VMEM((nz, NX, sub, CW), BF16),
            pltpu.VMEM((nz, NX, sub, CW), BF16),
            pltpu.VMEM((NX, nz, sub, CW), BF16),
            pltpu.VMEM((2, nz, sub, CW), BF16),
            pltpu.VMEM((2, nz // 2, sub, CW), BF16),
            pltpu.VMEM((nz, sub, CW), F32),
            pltpu.VMEM((nz, sub, CW), BF16),
            pltpu.VMEM((nz, sub, CW), BF16),
            pltpu.VMEM((2, sub // 2, CW), F32),
            pltpu.VMEM((sub // 2, CW), F32),
            pltpu.VMEM((tok, 2 * DN), BF16),
            pltpu.VMEM((tok, 2 * DR), BF16),
            pltpu.VMEM((tok, DL), BF16),
            pltpu.VMEM((DR, tok), BF16),
            pltpu.VMEM((sub // 2, 2 * DN), F32),
            pltpu.VMEM((sub // 2, 2 * DV), F32),
            dma((8,)), dma((6,)),
            dma((LAT_SUBS * (blocks + 1),)), dma((LAT_SUBS * (blocks + 1),)),
            dma((14,)), dma((2 * CORES * NX,)), dma((1,)), dma((1,)),
            dma((CORES * NX,)), dma((CORES * NX,)),
            dma((SUBS * blocks,)), dma((SUBS * blocks,)),
            dma((1,)), dma((1,)), dma((1,)), dma((1,)),
            dma((6,)), dma((6,)), dma((6,)), dma((6,)), dma((nz,)), dma((nz,)),
            dma((1,)), dma((1,)), dma((6,)), dma((2 * nyh,)),
            dma((1,)), dma((CORES,)), dma((1,)), dma((1,)),
        ]
        out_shape = (
            jax.ShapeDtypeStruct((1, tok, 2 * DN), BF16),
            jax.ShapeDtypeStruct((1, tok, 2 * DR), BF16),
            jax.ShapeDtypeStruct((1, tok, DL), BF16),
            jax.ShapeDtypeStruct((1, DR, tok), BF16),
            jax.ShapeDtypeStruct((sub // 2, 2 * DN), F32),
            jax.ShapeDtypeStruct((sub // 2, 2 * DV), F32),
        )
        results = pl.pallas_call(
            functools.partial(kernel, nz, nyh, tok),
            out_shape=out_shape,
            in_specs=[any_spec] * 8 + [pl.BlockSpec(memory_space=pltpu.SMEM)],
            out_specs=(any_spec,) * 6,
            scratch_shapes=scratch,
            compiler_params=pltpu.CompilerParams(
                collective_id=0, has_side_effects=True, vmem_limit_bytes=56 * 1024 * 1024
            ),
        )(args[0], jnp.swapaxes(args[1], 1, 2), *args[2:])
        results = pl.pallas_call(
            hand_over,
            out_shape=out_shape,
            in_specs=[vmem] * 6,
            out_specs=(vmem,) * 6,
        )(*results)
        return (*results[:3], jnp.swapaxes(results[3], 1, 2), *results[4:])

    return jax.shard_map(
        shards,
        mesh=mesh,
        in_specs=(
            P("dp", "ctx", None),
            P("dp", "ctx", None),
            P("dp", "ctx", "head"),
            P("dp", "ctx", "head"),
            P("dp", "ctx", "head"),
            P("dp", "ctx", "head"),
            P(None, "head"),
            P(None, "head"),
            P(),
        ),
        out_specs=(
            P("dp", "ctx", "head"),
            P("dp", "ctx", "head"),
            P("dp", "ctx", None),
            P("dp", "ctx", None),
            P(("ctx", "dp"), "head"),
            P(("ctx", "dp"), "head"),
        ),
        check_vma=False,
    )
```

```python
import functools
import math

import jax
import jax.numpy as jnp
from jax import lax
from jax.experimental import pallas as pl
from jax.experimental.pallas import tpu as pltpu
from jax.sharding import PartitionSpec as P

DL = 512
DN = 128
DR = 64
DV = 128
NX = 4
CORES = 2
HALF_GROUP = 64
LAT_SUBS = 4
SUBS = 4

QW = 2 * DN + 2 * DR + 2 * DV
KW = DN + 2 * DR
CW = 2 * DN + 2 * DV
LW = DL + 2 * DR
GW = 2 * DN + 2 * DR

MESH = pl.DeviceIdType.MESH
MASKED = -1.5e38
FLOOR = -1.0e38
F32 = jnp.float32
BF16 = jnp.bfloat16

NT = (((1,), (1,)), ((), ()))


def dot(a, b):
    return jnp.dot(a, b, preferred_element_type=F32)


def dot_nt(a, b):
    return lax.dot_general(a, b, NT, preferred_element_type=F32)


def kernel(
    nz, nyh, tok,
    lat_in, kr_in, qn_in, qr_in, go_in, so_in, wk_in, wv_in, order,
    gqn_out, gqr_out, gl_out, gkr_out, gwk_out, gwv_out,
    lat, krs, q, saved, w, qpos, qcat, qgo, latt, kcat, vals, keyst,
    pexp, dprob, mscr, lscr, stats, dsall, gall,
    glb, rsend, rrecv, tot, hsend, hsib, ybuf, final,
    gqf, gqsend, gqsib, gqb, gqr, gqfar, gwf, gwsend, gwsib, gwb, gwr, gwfar, gwzf, gwzb, gwzr, gwdf, gwdr,
    gqn_v, gqr_v, gl_v, gkr_v, gwk_v, gwv_v,
    local_sem, out_sem, lat_s, lat_r, q_s, q_r, w_s, w_r, st_s, st_r,
    rs_s, rs_r, gqs_s, gqs_r, gws_s, gws_r, gq_s, gq_r, gwx_s, gwx_r, gwz_s, gwz_r,
    half_s, half_r, y_s, y_r, fin_s, fin_r, dp_s, dp_r,
):
    ctx = lax.axis_index("ctx")
    head = lax.axis_index("head")
    dp = lax.axis_index("dp")
    z, x = lax.div(ctx, NX), lax.rem(ctx, NX)
    y, core = lax.div(head, CORES), lax.rem(head, CORES)
    queries = NX * tok
    blocks = nz // 2
    piece = tok // SUBS
    lat_piece = tok // LAT_SUBS
    half = tok // CORES
    score_scale = (DN + DR) ** -0.5
    log2_scale = score_scale * math.log2(math.e)
    sib_head = y * CORES + (1 - core)
    sib = 1 - core

    def at_z(peer):
        return {"ctx": peer * NX + x, "head": head, "dp": dp}

    def at_x(peer, head_index):
        return {"ctx": z * NX + peer, "head": head_index, "dp": dp}

    def at_head(peer):
        return {"ctx": ctx, "head": peer, "dp": dp}

    sibling = at_head(sib_head)
    other_dp = {"ctx": ctx, "head": head, "dp": 1 - dp}

    def remote(src, dst, send, recv, device):
        return pltpu.make_async_remote_copy(
            src_ref=src, dst_ref=dst, send_sem=send, recv_sem=recv,
            device_id=device, device_id_type=MESH,
        )

    def near(i, n):
        return [lax.rem(i + 1, n), lax.rem(i + n - 1, n)] if n > 2 else [1 - i]

    def others(i, n):
        return near(i, n) + [lax.rem(i + k, n) for k in range(2, n - 1)]

    z_peers, x_peers = others(z, nz), others(x, NX)
    x_near, y_near = near(x, NX), near(y, nyh)
    gather_to = at_z(lax.rem(z + (1 - core) * (nz - 1) + core, nz))
    sums_to = at_z(lax.rem(z + (1 - core) + core * (nz - 1), nz))
    y_devices = [at_head(p * CORES + core) for p in y_near]

    local = [
        pltpu.make_async_copy(lat_in.at[0], lat.at[0, :, pl.ds(0, DL)], local_sem.at[0]),
        pltpu.make_async_copy(kr_in.at[0], krs, local_sem.at[1]),
        pltpu.make_async_copy(qn_in.at[0], q.at[core, x, :, pl.ds(0, 2 * DN)], local_sem.at[2]),
        pltpu.make_async_copy(
            qr_in.at[0], q.at[core, x, :, pl.ds(2 * DN, 2 * DR)], local_sem.at[3]
        ),
        pltpu.make_async_copy(
            go_in.at[0], q.at[core, x, :, pl.ds(GW, 2 * DV)], local_sem.at[4]
        ),
        pltpu.make_async_copy(wk_in, w.at[core, :, pl.ds(0, 2 * DN)], local_sem.at[5]),
        pltpu.make_async_copy(wv_in, w.at[core, :, pl.ds(2 * DN, 2 * DV)], local_sem.at[6]),
        pltpu.make_async_copy(so_in.at[0], saved, local_sem.at[7]),
    ]
    barrier = pltpu.get_barrier_semaphore()
    targets = (
        [at_z(p) for p in near(z, nz)] + [at_x(p, head) for p in x_near]
        + [sibling, other_dp] + y_devices
    )
    for target in targets:
        pl.semaphore_signal(barrier, inc=1, device_id=target, device_id_type=MESH)
    for copy in local:
        copy.start()
    for copy in local[:2]:
        copy.wait()
    lat[0, :, DL:] = jnp.concatenate([krs[...].T, jnp.zeros((tok, DR), BF16)], axis=1)
    for copy in local[2:5]:
        copy.wait()
    pl.semaphore_wait(barrier, len(targets))

    def lat_copy(m, j):
        rows = pl.ds(j * lat_piece, lat_piece)
        return remote(
            lat.at[m, rows], lat.at[m + 1, rows], lat_s.at[m * LAT_SUBS + j],
            lat_r.at[(m + 1) * LAT_SUBS + j], gather_to,
        )

    def q_copy(p, j, send, device, c=core):
        rows = pl.ds(j * half, half)
        return remote(
            q.at[c, p, rows], q.at[c, p, rows], q_s.at[send], q_r.at[(c * NX + p) * 2 + j], device
        )

    sent = []

    def start(copy):
        copy.start()
        sent.append(copy)

    for j in range(LAT_SUBS):
        start(lat_copy(0, j))
    for j in range(2):
        for k, p in enumerate(x_near):
            start(q_copy(x, (j + k) % 2, 2 * k + j, at_x(p, head)))
    for copy in local[5:]:
        copy.wait()
    start(remote(w.at[core], w.at[core], w_s.at[0], w_r.at[0], sibling))
    for j in range(2):
        start(q_copy(x, j, 4 + j, sibling))

    product = (q[core, x, :, GW:].astype(F32) * saved[...].astype(F32)).T
    stats[core, x, 0:1, queries // 2:] = jnp.sum(product[:DV], axis=0, keepdims=True)
    stats[core, x, 1:2, queries // 2:] = jnp.sum(product[DV:], axis=0, keepdims=True)

    lane = lax.broadcasted_iota(jnp.int32, (1, tok), 1)
    for p in range(NX):
        first = 2 * (z * NX + p)
        qpos[0:1, p * tok:(p + 1) * tok] = jnp.where(
            lane < HALF_GROUP,
            order[first] * HALF_GROUP + lane,
            order[first + 1] * HALF_GROUP + lane - HALF_GROUP,
        )

    def pass_on(m):
        def take():
            for j in range(LAT_SUBS):
                lat_copy(m - 1, j).wait_recv()
                if m < blocks - 1:
                    start(lat_copy(m, j))
                elif m == blocks - 1:
                    @pl.when(core == 1)
                    def _():
                        lat_copy(m, j).start()

        if m < blocks:
            take()
        else:
            pl.when(core == 1)(take)

    def project(s):
        slot = s + core
        latents = lat[slot, :, 0:DL]
        rope = lat[slot, :, DL:]
        ropes = (rope, jnp.concatenate([rope[:, DR:], rope[:, :DR]], axis=1))
        columns = slice(s * tok, (s + 1) * tok)
        latt[:, columns] = latents.T
        for c in range(CORES):
            projected = dot(latents, w[c]).astype(BF16)
            for h in range(2):
                hh = 2 * c + h
                key = jnp.concatenate([projected[:, h * DN:(h + 1) * DN], ropes[h]], axis=1)
                kcat[hh, columns, :] = key
                keyst[hh, :, columns] = key.T
                vals[hh, columns, :] = projected[:, 2 * DN + h * DV:2 * DN + (h + 1) * DV]

    def q_take(p, j, number, onward=None):
        q_copy(p, j, 0, sibling).wait_recv()
        if onward is not None:
            start(q_copy(p, j, 6 + j, at_x(onward, head)))
        start(q_copy(p, j, 8 + number, sibling))

    def q_first():
        if len(x_near) == 2:
            right, left = x_near
            q_take(left, 0, 0, right)
            q_take(right, 1, 1, left)

    def q_second():
        if len(x_near) == 2:
            right, left = x_near
            q_take(left, 1, 2)
            q_take(right, 0, 3)
        else:
            for j in range(2):
                q_take(x_near[0], j, j)

    def q_third():
        for p in x_peers[2:]:
            for j in range(2):
                q_take(p, j, 4 + j)

    pass_on(1)
    remote(w.at[sib], w.at[sib], w_s.at[0], w_r.at[0], sibling).wait_recv()
    q_first()
    project(0)
    for s in range(1, max(blocks, 4)):
        if s == 3:
            q_third()
        if s < blocks:
            pass_on(s + 1)
        if s == 1:
            q_second()
        if s < blocks:
            project(s)
    for p in range(NX):
        for j in range(2):
            q_copy(p, j, 0, sibling, sib).wait_recv()
    for p in range(NX):
        rows = slice(p * tok, (p + 1) * tok)
        for c in range(CORES):
            for h in range(2):
                qcat[2 * c + h, rows, 0:DN] = q[c, p, :, h * DN:(h + 1) * DN]
                qcat[2 * c + h, rows, DN:] = q[c, p, :, 2 * DN:GW]
                qgo[2 * c + h, rows, :] = q[c, p, :, GW + h * DV:GW + (h + 1) * DV]

    def first_pass(s, carry):
        slot = s + core
        block = lax.rem(z + (1 - core) * slot + core * (nz - slot), nz)
        first = 2 * (block * NX + x)
        rows = pl.ds(pl.multiple_of(s * tok, tok), tok)
        row = lax.broadcasted_iota(jnp.int32, (HALF_GROUP, queries), 0)
        where_q = qpos[0:1, :]
        seen = jnp.concatenate(
            [row <= where_q - order[first + g] * HALF_GROUP for g in range(2)], axis=0
        )
        for hh in range(2 * CORES):
            scores = jnp.where(seen, dot_nt(kcat[hh, rows, :], qcat[hh]) * log2_scale, MASKED)
            top = jnp.maximum(jnp.max(scores, axis=0, keepdims=True), FLOOR)
            weight = jnp.exp2(scores - top)
            mscr[hh, s] = top
            lscr[hh, s] = jnp.sum(weight, axis=0, keepdims=True)
            pexp[hh, s] = weight
        return carry

    lax.fori_loop(0, blocks, first_pass, 0)

    for hh in range(2 * CORES):
        top = mscr[hh, 0]
        for s in range(1, blocks):
            top = jnp.maximum(top, mscr[hh, s])
        total = jnp.zeros_like(top)
        for s in range(blocks):
            total += lscr[hh, s] * jnp.exp2(mscr[hh, s] - top)
        summary = top + jnp.log2(jnp.maximum(total, 1e-37))
        stats[core, x, 2 * hh:2 * hh + 1, 0:queries // 2] = summary[:, :queries // 2]
        stats[core, x, 2 * hh + 1:2 * hh + 2, 0:queries // 2] = summary[:, queries // 2:]
    partners = []
    for p in reversed(x_peers):
        partners += [(core, p, at_x(p, head)), (sib, p, at_x(p, sib_head))]
    partners.append((sib, x, sibling))
    mine = core * NX + x
    for k, (_, _, device) in enumerate(partners):
        start(remote(stats.at[core, x], stats.at[core, x], st_s.at[k], st_r.at[mine], device))

    def cotangents(s, carry):
        rows = pl.ds(pl.multiple_of(s * tok, tok), tok)
        for hh in range(2 * CORES):
            dprob[hh, s] = dot_nt(vals[hh, rows, :], qgo[hh])
        return carry

    lax.fori_loop(0, blocks, cotangents, 0)
    for c, p, device in partners:
        remote(
            stats.at[c, p], stats.at[c, p], st_s.at[0], st_r.at[c * NX + p], device
        ).wait_recv()
    log_total, row_delta = [], []
    everyone = [(c, p) for c in range(CORES) for p in range(NX)]
    for hh in range(2 * CORES):
        sums = [
            jnp.concatenate(
                [stats[c, p, 2 * hh + k:2 * hh + k + 1, 0:queries // 2] for k in range(2)], axis=1
            )
            for c, p in everyone
        ]
        top = functools.reduce(jnp.maximum, sums)
        total = functools.reduce(jnp.add, [jnp.exp2(one - top) for one in sums])
        log_total.append(top + jnp.log2(total))
        row_delta.append(jnp.concatenate(
            [stats[hh // 2, p, hh % 2:hh % 2 + 1, queries // 2:] for p in range(NX)], axis=1
        ))

    def block_sums(t):
        s = blocks - 1 - t
        rows = slice(s * tok, (s + 1) * tok)
        ropes = []
        latent_sum = None
        for c in range(CORES):
            key_parts, value_parts = [], []
            for hh in (2 * c, 2 * c + 1):
                factor = jnp.exp2(mscr[hh, s] - log_total[hh])
                probs = pexp[hh, s] * factor
                dscores = (probs * ((dprob[hh, s] - row_delta[hh]) * score_scale)).astype(BF16)
                dsall[hh, rows, :] = dscores
                joint = dot(dscores, qcat[hh])
                key_parts.append(joint[:, :DN].astype(BF16))
                ropes.append(joint[:, DN:])
                value_parts.append(dot(probs.astype(BF16), qgo[hh]).astype(BF16))
            grads = jnp.concatenate(key_parts + value_parts, axis=1)
            gall[c, rows, :] = grads
            part = dot_nt(grads, w[c])
            latent_sum = part if latent_sum is None else latent_sum + part
        glb[t, :, 0:DL] = latent_sum
        glb[t, :, DL:] = jnp.where(
            lax.broadcasted_iota(jnp.int32, (tok, 2 * DR), 1) < DR,
            ropes[0] + ropes[2], ropes[1] + ropes[3],
        )

    def ring_copy(t, j):
        rows = pl.ds(j * piece, piece)
        return remote(
            rsend.at[t, rows], rrecv.at[t, rows], rs_s.at[t * SUBS + j], rs_r.at[t * SUBS + j],
            sums_to,
        )

    def ring_step(t):
        for j in range(SUBS):
            rows = slice(j * piece, (j + 1) * piece)
            so_far = glb[t, rows, :]
            if t > 0:
                ring_copy(t - 1, j).wait_recv()
                so_far = so_far + rrecv[t - 1, rows, :].astype(F32)
            rsend[t, rows, :] = so_far.astype(BF16)
            if t < blocks - 1:
                start(ring_copy(t, j))
            else:
                tot[rows, :] = so_far

                @pl.when(core == 1)
                def _():
                    ring_copy(t, j).start()

        if t == blocks - 1:
            @pl.when(core == 0)
            def _():
                hsend[...] = tot[half:, :].astype(BF16)
                for j in range(2):
                    half_copy(hsend.at[pl.ds(j * yhalf, yhalf)], j).start()

    yhalf = half // 2

    def half_copy(source, j):
        rows = pl.ds(j * yhalf, yhalf)
        return remote(source, hsib.at[rows], half_s.at[j], half_r.at[j], sibling)

    def query_grads(c):
        parts = [dot(keyst[2 * c + h], dsall[2 * c + h]) for h in range(2)]
        return jnp.concatenate(
            [parts[0][:DN], parts[1][:DN], parts[0][DN:] + parts[1][DN:]], axis=0
        ).T

    gq_pass = remote(gqsend, gqsib, gqs_s.at[0], gqs_r.at[0], sibling)
    gw_pass = remote(gwsend, gwsib, gws_s.at[0], gws_r.at[0], sibling)

    def sibling_query_grads():
        gqsend[...] = query_grads(sib).astype(BF16).reshape(gqsend.shape)
        start(gq_pass)

    def sibling_weight_grads():
        gwsend[...] = dot(latt[...], gall[sib]).astype(BF16).reshape(gwsend.shape)
        start(gw_pass)

    class Scatter:
        def __init__(self, blocks, arrived, far, send, recv):
            self.blocks, self.arrived, self.far = blocks, arrived, far
            self.send, self.recv = send, recv
            self.size = far.shape[1]

        def copy(self, src, dst, k, kind):
            return remote(
                src, dst, self.send.at[3 * k + kind], self.recv.at[3 * k + kind],
                at_x(x_near[k], head),
            )

        def part(self, ref, j):
            return ref.at[pl.ds(j * self.size, self.size)]

        def far_copy(self, k):
            return self.copy(
                self.part(self.blocks.at[lax.rem(x + 2, NX)], k), self.far.at[k], k, 0
            )

        def near_copy(self, k, kind):
            j = k if kind == 2 else 1 - k
            return self.copy(
                self.part(self.blocks.at[x_near[k]], j), self.part(self.arrived.at[k], j), k, kind
            )

        def begin(self):
            if len(x_near) == 2:
                for k in range(2):
                    start(self.far_copy(k))
            for k in range(len(x_near)):
                start(self.near_copy(k, 1))
                if len(x_near) == 1:
                    start(self.near_copy(k, 2))

        def pass_on(self):
            if len(x_near) == 2:
                for k in range(2):
                    self.far_copy(k).wait_recv()
                    rows = slice(k * self.size, (k + 1) * self.size)
                    p = x_near[k]
                    self.blocks[p, rows] = (
                        self.blocks[p, rows].astype(F32) + self.far[k].astype(F32)
                    ).astype(BF16)
                    start(self.near_copy(k, 2))

        def finish(self, own):
            for k in range(len(x_near)):
                for kind in (1, 2):
                    self.near_copy(k, kind).wait_recv()
                own += self.arrived[k].astype(F32)
            return own

    gw_scatter = Scatter(gwb, gwr, gwfar, gwx_s, gwx_r)
    gq_scatter = Scatter(gqb, gqr, gqfar, gq_s, gq_r)

    def own_weight_grads():
        gwf[...] = dot(latt[...], gall[core]).reshape(gwf.shape)
        gw_pass.wait_recv()
        gwf[...] += gwsib[...].astype(F32)
        for p in range(NX):
            gwb[p] = gwf[:, p].astype(BF16)
        gw_scatter.begin()

    def own_query_grads():
        own_queries = query_grads(core).reshape(gqf.shape)
        gq_pass.wait_recv()
        gqf[...] = own_queries + gqsib[...].astype(F32)
        gqb[...] = gqf[...].astype(BF16)

    between = [
        [functools.partial(block_sums, t) for t in range(1, blocks)] + [sibling_weight_grads],
        [sibling_query_grads, own_weight_grads], [own_query_grads],
    ]
    block_sums(0)
    ring_step(0)
    for t in range(1, blocks):
        for item in between.pop(0):
            item()
        ring_step(t)
    for item in sum(between, []):
        item()
    gw_scatter.pass_on()
    gq_scatter.begin()

    def y_copy(slot, j, send, device):
        rows = pl.ds(j * yhalf, yhalf)
        return remote(
            ybuf.at[slot, rows], ybuf.at[slot, rows], y_s.at[send], y_r.at[2 * slot + j], device
        )

    def last_pieces(j):
        for k in range(j * SUBS // 4, (j + 1) * SUBS // 4):
            ring_copy(blocks - 1, k).wait_recv()

    @pl.when(core == 1)
    def _():
        for j in range(2):
            last_pieces(j)
            half_copy(rrecv.at[blocks - 1, pl.ds(j * yhalf, yhalf)], j).start()

    for j in range(2):
        @pl.when(core == 1)
        def _():
            last_pieces(2 + j)
            rows = slice(half + j * yhalf, half + (j + 1) * yhalf)
            tot[rows, :] = rrecv[blocks - 1, rows, :].astype(F32)

        rows = slice(j * yhalf, (j + 1) * yhalf)
        half_copy(hsend.at[pl.ds(j * yhalf, yhalf)], j).wait_recv()
        mine_now = tot[pl.ds(pl.multiple_of(core * half + j * yhalf, yhalf), yhalf), :]
        ybuf[y, rows, :] = (mine_now + hsib[rows, :].astype(F32)).astype(BF16)
        if len(y_devices) == 2:
            start(y_copy(y, j, j, y_devices[j]))
        else:
            start(y_copy(y, j, j, y_devices[0]))
    if len(y_devices) == 2:
        for j in range(2):
            start(y_copy(y, j, 2 + j, y_devices[1 - j]))

    part = gw_scatter.finish(gwf[:, x])
    gwzf[...] = part
    gwzb[...] = part.astype(BF16)
    for k, p in enumerate(reversed(z_peers)):
        start(remote(gwzb.at[p], gwzr.at[z], gwz_s.at[k], gwz_r.at[z], at_z(p)))

    gq_scatter.pass_on()
    if nyh > 2:
        right, left = y_near
        y_copy(left, 0, 0, sibling).wait_recv()
        start(y_copy(left, 0, 4, y_devices[0]))
        y_copy(right, 1, 0, sibling).wait_recv()
        start(y_copy(right, 1, 5, y_devices[1]))

    part = gq_scatter.finish(gqf[x])
    gqn_v[...] = part[:, :2 * DN].astype(BF16)
    gqr_v[...] = part[:, 2 * DN:].astype(BF16)
    out_copies = [
        pltpu.make_async_copy(gqn_v, gqn_out.at[0], out_sem.at[0]),
        pltpu.make_async_copy(gqr_v, gqr_out.at[0], out_sem.at[1]),
        pltpu.make_async_copy(gl_v, gl_out.at[0], out_sem.at[2]),
        pltpu.make_async_copy(gkr_v, gkr_out.at[0], out_sem.at[3]),
        pltpu.make_async_copy(gwk_v, gwk_out, out_sem.at[4]),
        pltpu.make_async_copy(gwv_v, gwv_out, out_sem.at[5]),
    ]
    for copy in out_copies[:2]:
        copy.start()

    part = gwzf[z]
    for p in z_peers:
        remote(gwzb.at[0], gwzr.at[p], gwz_s.at[0], gwz_r.at[p], at_z(p)).wait_recv()
        part += gwzr[p].astype(F32)
    gwdf[...] = part.reshape(gwdf.shape)
    dp_copy = remote(gwdf.at[1 - dp], gwdr, dp_s.at[0], dp_r.at[0], other_dp)
    start(dp_copy)

    if nyh > 2:
        y_copy(left, 1, 0, sibling).wait_recv()
        y_copy(right, 0, 0, sibling).wait_recv()
        far = others(y, nyh)[2]
        for j in range(2):
            y_copy(far, j, 0, sibling).wait_recv()
    else:
        for j in range(2):
            y_copy(y_near[0], j, 0, sibling).wait_recv()
    part = functools.reduce(jnp.add, [ybuf[k].astype(F32) for k in range(nyh)])
    folded = part[:, DL:] + jnp.concatenate([part[:, DL + DR:], part[:, DL:DL + DR]], axis=1)
    final[core, :, 0:DL] = part[:, :DL].astype(BF16)
    final[core, :, DL:] = folded.astype(BF16)
    start(remote(final.at[core], final.at[core], fin_s.at[0], fin_r.at[core], sibling))

    dp_copy.wait_recv()
    summed = gwdf[dp] + gwdr[...]
    gwk_v[...] = summed[:, :2 * DN]
    gwv_v[...] = summed[:, 2 * DN:]
    for copy in out_copies[4:]:
        copy.start()

    remote(final.at[sib], final.at[sib], fin_s.at[0], fin_r.at[sib], sibling).wait_recv()
    gl_v[...] = jnp.concatenate([final[c, :, 0:DL] for c in range(CORES)], axis=0)
    gkr_v[...] = jnp.concatenate([final[c, :, DL:] for c in range(CORES)], axis=0).T[:DR]
    for copy in out_copies[2:4]:
        copy.start()

    for copy in sent:
        copy.wait_send()
    for j in range(2):
        half_copy(hsend.at[pl.ds(j * yhalf, yhalf)], j).wait_send()

    @pl.when(core == 1)
    def _():
        for j in range(LAT_SUBS):
            lat_copy(blocks - 1, j).wait_send()
        for j in range(SUBS):
            ring_copy(blocks - 1, j).wait_send()

    for copy in out_copies:
        copy.wait()


def hand_over(*refs):
    count = len(refs) // 2
    for k in range(count):
        refs[count + k][...] = refs[k][...]


def solution(mesh):
    nz = mesh.shape["ctx"] // NX
    nyh = mesh.shape["head"] // CORES

    def shards(*args):
        tok = args[0].shape[1]
        queries = NX * tok
        blocks = nz // 2
        keys = blocks * tok
        sub = DL // (nz * NX)
        any_spec = pl.BlockSpec(memory_space=pl.ANY)
        vmem = pl.BlockSpec(memory_space=pltpu.VMEM)
        dma = pltpu.SemaphoreType.DMA
        scratch = [
            pltpu.VMEM((blocks + 1, tok, LW), BF16),
            pltpu.VMEM((DR, tok), BF16),
            pltpu.VMEM((CORES, NX, tok, QW), BF16),
            pltpu.VMEM((tok, 2 * DV), BF16),
            pltpu.VMEM((CORES, DL, CW), BF16),
            pltpu.VMEM((8, queries), jnp.int32),
            pltpu.VMEM((4, queries, KW), BF16),
            pltpu.VMEM((4, queries, DV), BF16),
            pltpu.VMEM((DL, keys), BF16),
            pltpu.VMEM((4, keys, KW), BF16),
            pltpu.VMEM((4, keys, DV), BF16),
            pltpu.VMEM((4, KW, keys), BF16),
            pltpu.VMEM((4, blocks, tok, queries), F32),
            pltpu.VMEM((4, blocks, tok, queries), F32),
            pltpu.VMEM((4, blocks, 1, queries), F32),
            pltpu.VMEM((4, blocks, 1, queries), F32),
            pltpu.VMEM((CORES, NX, 8, queries // 2 + tok), F32),
            pltpu.VMEM((4, keys, queries), BF16),
            pltpu.VMEM((CORES, keys, CW), BF16),
            pltpu.VMEM((blocks, tok, LW), F32),
            pltpu.VMEM((blocks, tok, LW), BF16),
            pltpu.VMEM((blocks, tok, LW), BF16),
            pltpu.VMEM((tok, LW), F32),
            pltpu.VMEM((tok // CORES, LW), BF16),
            pltpu.VMEM((tok // CORES, LW), BF16),
            pltpu.VMEM((nyh, tok // CORES, LW), BF16),
            pltpu.VMEM((CORES, tok // CORES, LW), BF16),
            pltpu.VMEM((NX, tok, GW), F32),
            pltpu.VMEM((NX, tok, GW), BF16),
            pltpu.VMEM((NX, tok, GW), BF16),
            pltpu.VMEM((NX, tok, GW), BF16),
            pltpu.VMEM((2, tok, GW), BF16),
            pltpu.VMEM((2, tok // 2, GW), BF16),
            pltpu.VMEM((nz, NX, sub, CW), F32),
            pltpu.VMEM((nz, NX, sub, CW), BF16),
            pltpu.VMEM((nz, NX, sub, CW), BF16),
            pltpu.VMEM((NX, nz, sub, CW), BF16),
            pltpu.VMEM((2, nz, sub, CW), BF16),
            pltpu.VMEM((2, nz // 2, sub, CW), BF16),
            pltpu.VMEM((nz, sub, CW), F32),
            pltpu.VMEM((nz, sub, CW), BF16),
            pltpu.VMEM((nz, sub, CW), BF16),
            pltpu.VMEM((2, sub // 2, CW), F32),
            pltpu.VMEM((sub // 2, CW), F32),
            pltpu.VMEM((tok, 2 * DN), BF16),
            pltpu.VMEM((tok, 2 * DR), BF16),
            pltpu.VMEM((tok, DL), BF16),
            pltpu.VMEM((DR, tok), BF16),
            pltpu.VMEM((sub // 2, 2 * DN), F32),
            pltpu.VMEM((sub // 2, 2 * DV), F32),
            dma((8,)), dma((6,)),
            dma((LAT_SUBS * (blocks + 1),)), dma((LAT_SUBS * (blocks + 1),)),
            dma((14,)), dma((2 * CORES * NX,)), dma((1,)), dma((1,)),
            dma((CORES * NX,)), dma((CORES * NX,)),
            dma((SUBS * blocks,)), dma((SUBS * blocks,)),
            dma((1,)), dma((1,)), dma((1,)), dma((1,)),
            dma((6,)), dma((6,)), dma((6,)), dma((6,)), dma((nz,)), dma((nz,)),
            dma((2,)), dma((2,)), dma((6,)), dma((2 * nyh,)),
            dma((1,)), dma((CORES,)), dma((1,)), dma((1,)),
        ]
        out_shape = (
            jax.ShapeDtypeStruct((1, tok, 2 * DN), BF16),
            jax.ShapeDtypeStruct((1, tok, 2 * DR), BF16),
            jax.ShapeDtypeStruct((1, tok, DL), BF16),
            jax.ShapeDtypeStruct((1, DR, tok), BF16),
            jax.ShapeDtypeStruct((sub // 2, 2 * DN), F32),
            jax.ShapeDtypeStruct((sub // 2, 2 * DV), F32),
        )
        results = pl.pallas_call(
            functools.partial(kernel, nz, nyh, tok),
            out_shape=out_shape,
            in_specs=[any_spec] * 8 + [pl.BlockSpec(memory_space=pltpu.SMEM)],
            out_specs=(any_spec,) * 6,
            scratch_shapes=scratch,
            compiler_params=pltpu.CompilerParams(
                collective_id=0, has_side_effects=True, vmem_limit_bytes=56 * 1024 * 1024
            ),
        )(args[0], jnp.swapaxes(args[1], 1, 2), *args[2:])
        results = pl.pallas_call(
            hand_over,
            out_shape=out_shape,
            in_specs=[vmem] * 6,
            out_specs=(vmem,) * 6,
        )(*results)
        return (*results[:3], jnp.swapaxes(results[3], 1, 2), *results[4:])

    return jax.shard_map(
        shards,
        mesh=mesh,
        in_specs=(
            P("dp", "ctx", None),
            P("dp", "ctx", None),
            P("dp", "ctx", "head"),
            P("dp", "ctx", "head"),
            P("dp", "ctx", "head"),
            P("dp", "ctx", "head"),
            P(None, "head"),
            P(None, "head"),
            P(),
        ),
        out_specs=(
            P("dp", "ctx", "head"),
            P("dp", "ctx", "head"),
            P("dp", "ctx", None),
            P("dp", "ctx", None),
            P(("ctx", "dp"), "head"),
            P(("ctx", "dp"), "head"),
        ),
        check_vma=False,
    )
```
